32 devices in a mesh: seq: 8 (over z, y), rep: 4 (over x, core).
Axes of the slice: x: 2, y: 2, z: 4, core: 2. Of those that a mesh axis runs over, the one named last changes fastest.
Arguments:
- points: bfloat16 [4096, 512], P(('rep', 'seq')), parts along dimension 0, may hold values from -6 to 6
- decay_one: float32 [8, 4096], P(None, ('rep', 'seq')), parts along dimension 1, may hold values from -1 to 0
- decay_two: float32 [8, 8192], P(None, ('rep', 'seq')), parts along dimension 1, may hold values from -1 to 0
- block_target: int32 [512], P('rep'), parts along dimension 0, may hold values from 0 to 255, as said below
- w_qkv_one: bfloat16 [512, 1536], replicated, may hold values from -0.25 to 0.25
- w_out_one: bfloat16 [512, 512], replicated, may hold values from -0.25 to 0.25
- w_up: bfloat16 [512, 2048], P(None, 'seq'), may hold values from -0.25 to 0.25
- w_down: bfloat16 [2048, 512], P('seq'), may hold values from -0.125 to 0.125
- w_qkv_two: bfloat16 [512, 1536], replicated, may hold values from -0.25 to 0.25
- w_out_two: bfloat16 [512, 512], replicated, may hold values from -0.25 to 0.25
Outputs:
- mixed: bfloat16 [8192, 512], P(('rep', 'seq')), parts along dimension 0
The draws below stay inside these ranges and needn't reach their ends.
There are 4 independent parts, one for each index of `rep`. The reference program is written for one: setup_inputs(seed, part) draws one part's arguments, and reference() takes and returns one part's arrays. A program takes and returns all parts, laid end to end along the dimension named above; an argument that names none is the same for every part. Nothing has to cross between parts.
Inputs may be any that keep to these rules, and one draw needn't show every extreme that they name: `block_target`: entry b is the slot of block b of points; slot g is position g % 32 on device g // 32 of seq, and slots in increasing order give the second sequence. Entries are distinct, every device uses its first slots only, and some device uses all 32. Taken in slot order the blocks go column by column: for one local index j, the j-th block of every device in increasing device order, the columns in some order. At most 4 blocks of one device go to one device, and some device sends that many to one device.
All inputs are finite; a program needn't handle non-finite values.
Results may differ from the reference program's by a relative error of at most 0.018.
Values may be sent and summed in bfloat16 or wider, within the bound.
A program may use at most 128 MiB of HBM per device.

```python
import math
import jax
import jax.numpy as jnp
from jax import lax

D = 512
MIXER_STREAMS = 8
HEAD_DIM = 64
FF = 2048
BR = 8
TOK_DEV = 128
BLK_DEV = 16
CAP = 32
TOKENS = 1024
NBLK = 128
SLOTS = 256


def decay_law(key, overall_span, group):
    matching_rows = jax.random.split(jax.random.fold_in(key, 7), 8)
    order = jax.random.permutation(matching_rows[0], MIXER_STREAMS)
    slow_count = MIXER_STREAMS // 2
    slow = jnp.zeros((MIXER_STREAMS,), jnp.int32).at[order[:slow_count]].set(1) > 0
    slow_rate = jnp.exp(jax.random.uniform(matching_rows[1], (MIXER_STREAMS,), jnp.float32, math.log(0.08), math.log(0.2))) * math.log(10.0) / TOKENS
    fast_rate = jnp.exp(jax.random.uniform(matching_rows[2], (MIXER_STREAMS,), jnp.float32, math.log(1.0 / 50.0), math.log(1.0 / 30.0)))
    forgetting_rate = jnp.where(slow, slow_rate, fast_rate)
    rough_guess = jax.random.uniform(matching_rows[3], (MIXER_STREAMS, overall_span), jnp.float32, 0.5, 1.5)
    processor_scaling = jnp.exp(jax.random.uniform(matching_rows[4], (overall_span // group,), jnp.float32, math.log(0.6), math.log(1.8)))
    processor_scaling = jnp.repeat(processor_scaling, group)
    initial_bundle = jax.random.randint(matching_rows[5], (MIXER_STREAMS, 1), 0, overall_span)
    subsequent_bundle = (initial_bundle + 1 + jax.random.randint(matching_rows[6], (MIXER_STREAMS, 1), 0, overall_span - 1)) % overall_span
    level_count = jnp.log(jax.random.uniform(matching_rows[7], (MIXER_STREAMS, 2), jnp.float32, 0.5, 0.8))
    position_numbers = lax.broadcasted_iota(jnp.int32, (MIXER_STREAMS, overall_span), 1)
    message_bundles = jnp.where(position_numbers == initial_bundle, level_count[:, :1], 0.0) + jnp.where(position_numbers == subsequent_bundle, level_count[:, 1:], 0.0)
    return -forgetting_rate[:, None] * rough_guess * processor_scaling[None, :] + message_bundles


def draw_decay_one(key, part):
    return decay_law(key, TOKENS, TOK_DEV)


def draw_decay_two(key, part):
    return decay_law(jax.random.fold_in(key, 3), SLOTS * BR, CAP * BR)


def draw_block_target(key, part):
    matching_rows = jax.random.split(jax.random.fold_in(key, 5), 3)
    seq_count = NBLK // BLK_DEV
    column_order = jax.random.permutation(matching_rows[0], BLK_DEV)
    column_rank = jnp.argsort(column_order).astype(jnp.int32)
    pairing = jax.random.permutation(matching_rows[1], seq_count)
    shifts = jax.random.randint(matching_rows[2], (seq_count // 2,), 0, BLK_DEV + 1).at[0].set(BLK_DEV)
    lengths = jnp.zeros((seq_count,), jnp.int32).at[pairing[0::2]].set(BLK_DEV + shifts).at[pairing[1::2]].set(BLK_DEV - shifts)
    ends = jnp.cumsum(lengths)
    starts = ends - lengths
    order_pos = jnp.arange(NBLK, dtype=jnp.int32)
    owner = jnp.sum((ends[None, :] <= order_pos[:, None]).astype(jnp.int32), axis=1)
    slot_of = owner * CAP + order_pos - starts[owner]
    blocks = jnp.arange(NBLK, dtype=jnp.int32)
    where_in = column_rank[blocks % BLK_DEV] * seq_count + blocks // BLK_DEV
    return slot_of[where_in].astype(jnp.int32)


def level_of(key, dims, cuts, least, high):
    def one(position, shards_of):
        draws = jax.random.uniform(jax.random.fold_in(jax.random.fold_in(key, 6), position), (shards_of,), jnp.float32, least / len(cuts), high / len(cuts))
        return jnp.repeat(jnp.exp(draws), dims[position] // shards_of).reshape((-1,) + (1,) * (len(dims) - position - 1))

    loudness = one(*cuts[0])
    for cut in cuts[1:]:
        loudness = loudness * one(*cut)
    return loudness


def centred(own_key, extent, scale, reach, cuts=(), held_as=jnp.bfloat16):
    result = jax.random.normal(own_key, extent, jnp.float32) * scale
    if len(cuts) > 0:
        result = level_of(own_key, extent, cuts, -0.22, 0.18) * result
    return jnp.clip(result, min=-reach, max=reach).astype(held_as)


def setup_inputs(seed: int = 0, part: int = 0) -> dict:
    key_list = jax.random.split(jax.random.key(seed), 11)
    part_splits = jax.random.split(jax.random.fold_in(key_list[10], part), 11)
    return {
        "points": centred(part_splits[0], (TOKENS, D), 1.0, 6.0, ((0, 8),)),
        "decay_one": draw_decay_one(jax.random.fold_in(jax.random.fold_in(key_list[10], part), 71), part),
        "decay_two": draw_decay_two(jax.random.fold_in(jax.random.fold_in(key_list[10], part), 71), part),
        "block_target": draw_block_target(jax.random.fold_in(jax.random.fold_in(key_list[10], part), 71), part),
        "w_qkv_one": centred(key_list[4], (D, 3 * D), D ** -0.5, 0.25),
        "w_out_one": centred(key_list[5], (D, D), D ** -0.5, 0.25),
        "w_up": centred(key_list[6], (D, FF), D ** -0.5, 0.25, ((1, 8),)),
        "w_down": centred(key_list[7], (FF, D), FF ** -0.5, 0.125, ((0, 8),)),
        "w_qkv_two": centred(key_list[8], (D, 3 * D), D ** -0.5, 0.25),
        "w_out_two": centred(key_list[9], (D, D), D ** -0.5, 0.25),
    }


epsilon = 1e-05
highest = lax.Precision.HIGHEST

def rms_rows(inputs):
    wide = inputs.astype(jnp.float32)
    return wide * lax.rsqrt(lax.optimization_barrier(jnp.mean(wide * wide, axis=-1, keepdims=True)) + epsilon)

def project(inputs, weight):
    normed = rms_rows(inputs).astype(jnp.bfloat16)
    joined = jnp.dot(normed, weight, preferred_element_type=jnp.float32)
    column = lax.broadcasted_iota(jnp.int32, (1, 3 * D), 1)
    scaled = jnp.where(column < D, joined * HEAD_DIM ** (-0.5), joined)
    return scaled.astype(jnp.bfloat16)

def block_summary(key_rows, values, decay):
    cumulative = jnp.cumsum(decay, axis=1)
    decay_total = cumulative[:, -1]
    weighted = key_rows.astype(jnp.float32) * jnp.exp(decay_total[:, None] - cumulative)[:, :, None]
    state_sum = jnp.einsum('hsd,hse->hde', weighted, values.astype(jnp.float32), precision=highest)
    return (cumulative, decay_total, state_sum)

def block_output(queries, key_rows, values, cumulative, entering):
    span = queries.shape[1]
    causal = (lax.broadcasted_iota(jnp.int32, (span, span), 0) >= lax.broadcasted_iota(jnp.int32, (span, span), 1))[None]
    gap = cumulative[:, :, None] - cumulative[:, None, :]
    weight = jnp.where(causal, jnp.exp(jnp.where(causal, gap, 0.0)), 0.0)
    scores = jnp.einsum('htd,hsd->hts', queries.astype(jnp.float32), key_rows.astype(jnp.float32))
    weighted = (scores * weight).astype(jnp.bfloat16)
    inner = jnp.einsum('hts,hse->hte', weighted.astype(jnp.float32), values.astype(jnp.float32))
    carried = jnp.einsum('htd,hde->hte', queries.astype(jnp.float32), entering, precision=highest)
    summed = inner + carried * jnp.exp(cumulative)[:, :, None]
    return summed * lax.rsqrt(lax.optimization_barrier(jnp.mean(summed * summed, axis=-1, keepdims=True)) + epsilon)

def attend_all(joined, decay):
    total_rows = joined.shape[0]
    span = math.gcd(total_rows, 512)
    count = total_rows // span

    def heads_blocks(matrix):
        return matrix.reshape(count, span, MIXER_STREAMS, HEAD_DIM).transpose(0, 2, 1, 3)
    queries = heads_blocks(joined[:, :D])
    key_rows = heads_blocks(joined[:, D:2 * D])
    values = heads_blocks(joined[:, 2 * D:])
    decay_blocks = decay.reshape(MIXER_STREAMS, count, span).transpose(1, 0, 2)

    def advance(carry, pieces):
        query_block, key_block, value_block, decay_block = pieces
        cumulative, decay_total, state_sum = block_summary(key_block, value_block, decay_block)
        output = block_output(query_block, key_block, value_block, cumulative, carry)
        carry = carry * jnp.exp(decay_total)[:, None, None] + state_sum
        return (carry, output.astype(jnp.bfloat16))
    start = jnp.zeros((MIXER_STREAMS, HEAD_DIM, HEAD_DIM), jnp.float32)
    _, outputs = lax.scan(advance, start, (queries, key_rows, values, decay_blocks))
    return outputs.transpose(0, 2, 1, 3).reshape(total_rows, D)

def reference(points, decay_one, decay_two, block_target, w_qkv_one, w_out_one, w_up, w_down, w_qkv_two, w_out_two):
    joined = project(points, w_qkv_one)
    attended = attend_all(joined, decay_one)
    first = (points.astype(jnp.float32) + jnp.dot(attended, w_out_one, preferred_element_type=jnp.float32)).astype(jnp.bfloat16)
    normed = rms_rows(first).astype(jnp.bfloat16)
    hidden = jax.nn.gelu(jnp.dot(normed, w_up, preferred_element_type=jnp.float32), approximate=True).astype(jnp.bfloat16)
    layer_out = (first.astype(jnp.float32) + jnp.dot(hidden, w_down, preferred_element_type=jnp.float32)).astype(jnp.bfloat16)
    blocks = layer_out.reshape(NBLK, BR, D)
    placed = jnp.zeros((SLOTS, BR, D), jnp.bfloat16).at[block_target].set(blocks).reshape(SLOTS * BR, D)
    used = jnp.zeros((SLOTS,), jnp.float32).at[block_target].set(1.0)
    decay_mask = jnp.repeat(used, BR)
    joined_two = project(placed, w_qkv_two)
    attended_two = attend_all(joined_two, decay_two * decay_mask[None, :])
    return (placed.astype(jnp.float32) + jnp.dot(attended_two, w_out_two, preferred_element_type=jnp.float32)).astype(jnp.bfloat16)
```

```python
import functools

import jax
import jax.numpy as jnp
from jax import lax
from jax.experimental import pallas as pl
from jax.experimental.pallas import tpu as pltpu
from jax.sharding import PartitionSpec as P

MIXER_STREAMS = 8
HEAD_DIM = 64
BR = 8
CAP = 32
LANES = 128
EPS = 1e-05
F32 = jnp.float32
BF16 = jnp.bfloat16
MESH = pl.DeviceIdType.MESH
UNROLL = 16


def dot(a, b):
    return jnp.dot(a, b, preferred_element_type=F32)


def dot_nt(a, b):
    return lax.dot_general(a, b, (((1,), (1,)), ((), ())), preferred_element_type=F32)


def dot_tn(a, b):
    return lax.dot_general(a, b, (((0,), (0,)), ((), ())), preferred_element_type=F32)


def iota(shape, dim):
    return lax.broadcasted_iota(jnp.int32, shape, dim)


def ones_where(mask):
    return jnp.where(mask, 1.0, 0.0).astype(BF16)


def split3(x):
    hi = x.astype(BF16)
    rest = x - hi.astype(F32)
    mid = rest.astype(BF16)
    low = (rest - mid.astype(F32)).astype(BF16)
    return hi, mid, low


def rms(x):
    return x * lax.rsqrt(jnp.mean(x * x, axis=-1, keepdims=True) + EPS)


def gelu(x):
    return 0.5 * x * (1.0 + jnp.tanh(0.7978845608028654 * (x + 0.044715 * (x * x * x))))


def loop(start, stop, body):
    if stop - start <= UNROLL:
        for i in range(start, stop):
            body(i)
    else:
        def step(i, carry):
            body(i)
            return carry

        lax.fori_loop(start, stop, step, 0)


def log2(n):
    assert n & (n - 1) == 0
    return n.bit_length() - 1


def project(x, weight, joined):
    width = x.shape[1]
    normed = rms(x).astype(BF16)
    joined[:, :width] = (dot(normed, weight[:, :width]) * HEAD_DIM**-0.5).astype(BF16)
    joined[:, width:] = dot(normed, weight[:, width:]).astype(BF16)


def kernel(
    seq, reps, owners,
    points, decay_one, decay_two, target, w_qkv_one, w_out_one, w_up, w_down, w_qkv_two, w_out_two,
    out,
    wq1, wo1, wq2, wo2, up, down,
    joined_one, joined_two, num_one, num_two, att_one, att_two,
    a_send, a_recv, b_send, b_recv, blk_send, blk_recv, acc,
    load_sem, own_sem, ring_send, ring_recv, core_send, core_recv,
    ex_send, ex_recv,
):
    me = lax.axis_index("seq")
    rep = lax.axis_index("rep")
    rows, width = points.shape
    rows_two = out.shape[0]
    half = seq // 2
    halves = 2 if reps % 2 == 0 else 1
    part = width // halves
    mine = rep % halves
    partner = rep + 1 - 2 * (rep % 2)
    groups = width // LANES
    per_group = owners // groups
    state_rows = HEAD_DIM // per_group
    pair_rows = blk_send.shape[1]

    loads = [
        pltpu.make_async_copy(src, dst, load_sem.at[i])
        for i, (src, dst) in enumerate(
            ((w_qkv_one, wq1), (w_out_one, wo1), (w_qkv_two, wq2), (w_out_two, wo2))
        )
    ]
    loads[0].start()
    own = [
        pltpu.make_async_copy(w_up, up.at[me], own_sem.at[0]),
        pltpu.make_async_copy(w_down, down.at[me], own_sem.at[1]),
    ]

    barrier = pltpu.get_barrier_semaphore()

    def greet(i):
        pl.semaphore_signal(
            barrier, inc=1, device_id={"seq": lax.rem(me + i, seq)}, device_id_type=MESH
        )

    loop(1, seq, greet)
    if halves == 2:
        pl.semaphore_signal(barrier, inc=1, device_id={"rep": partner}, device_id_type=MESH)
    pl.semaphore_wait(barrier, seq - 1 + (1 if halves == 2 else 0))

    place = jnp.where(me % 2 == 0, me // 2, seq - 1 - me // 2)

    def at_place(p):
        q = lax.rem(p + 2 * seq, seq)
        return jnp.where(q < half, 2 * q, 2 * (seq - 1 - q) + 1)

    neighbour = (at_place(place + 1), at_place(place - 1))

    def piece(w, s):
        if w == 0:
            return up.at[s, pl.ds(pl.multiple_of(mine * part, part), part), :]
        return down.at[s, :, pl.ds(pl.multiple_of(mine * part, part), part)]

    def own_piece(w):
        if w == 0:
            return w_up.at[pl.ds(pl.multiple_of(mine * part, part), part), :]
        return w_down.at[:, pl.ds(pl.multiple_of(mine * part, part), part)]

    def origin(way, k):
        return at_place(place - k if way == 0 else place + k)

    def ring(way, w, k, first=False):
        where = piece(w, me if first else origin(way, k - 1))
        return pltpu.make_async_remote_copy(
            src_ref=own_piece(w) if first else where,
            dst_ref=where,
            send_sem=ring_send.at[way, w, k - 1],
            recv_sem=ring_recv.at[way, w, k - 1],
            device_id={"seq": neighbour[way]},
            device_id_type=MESH,
        )

    def ring_arrival(way, w, k):
        where = piece(w, origin(way, k))
        return pltpu.make_async_remote_copy(
            src_ref=where,
            dst_ref=where,
            send_sem=ring_send.at[way, w, k - 1],
            recv_sem=ring_recv.at[way, w, k - 1],
            device_id={"seq": neighbour[way]},
            device_id_type=MESH,
        )

    def core(way, w, k):
        where = piece(w, origin(way, k))
        return pltpu.make_async_remote_copy(
            src_ref=where,
            dst_ref=where,
            send_sem=core_send.at[way, w, k - 1],
            recv_sem=core_recv.at[way, w, k - 1],
            device_id={"rep": partner},
            device_id_type=MESH,
        )

    both = [(way, w) for w in range(2) for way in range(2)]
    last = [(0, 0), (1, 1)]

    def routes(k):
        return last if isinstance(k, int) and k == half else both

    def relay(k, routes_now, routes_next):
        for way, w in routes_now:
            ring_arrival(way, w, k).wait_recv()
            if (way, w) in routes_next:
                ring(way, w, k + 1).start()
            if halves == 2:
                core(way, w, k).start()

    def relay_step(k):
        relay(k, routes(k), routes(k + 1) if k < half else [])

    for way, w in routes(1):
        ring(way, w, 1, first=True).start()
    for copy in loads[1:] + own:
        copy.start()

    def exchange(index, source, target_buf, count):
        def copy(i, peer):
            return pltpu.make_async_remote_copy(
                src_ref=source.at[peer],
                dst_ref=target_buf.at[me],
                send_sem=ex_send.at[index, i],
                recv_sem=ex_recv.at[index, i],
                device_id={"seq": peer},
                device_id_type=MESH,
            )

        def arrival(i):
            src = lax.rem(me - i + seq, seq)
            return pltpu.make_async_remote_copy(
                src_ref=target_buf.at[src],
                dst_ref=target_buf.at[src],
                send_sem=ex_send.at[index, i],
                recv_sem=ex_recv.at[index, i],
                device_id={"seq": lax.rem(me + i, seq)},
                device_id_type=MESH,
            )

        return copy, arrival

    def maybe(cond, all_true, body):
        if all_true:
            body()
        else:
            pl.when(cond)(body)

    def to_owners(index, layer):
        copy, arrival = exchange(index, a_send.at[layer], a_recv.at[layer], owners)

        def start(i):
            peer = lax.rem(me + i, seq)
            maybe(peer < owners, owners == seq, lambda: copy(i, peer).start())

        def finish(i):
            peer = lax.rem(me + i, seq)
            maybe(me < owners, owners == seq, lambda: arrival(i).wait_recv())

        def sent(i):
            peer = lax.rem(me + i, seq)
            maybe(peer < owners, owners == seq, lambda: copy(i, peer).wait_send())

        return start, finish, sent

    def from_owners(index, layer):
        copy, arrival = exchange(index, b_send.at[layer], b_recv.at[layer], seq)

        def start(i):
            peer = lax.rem(me + i, seq)
            maybe(me < owners, owners == seq, lambda: copy(i, peer).start())

        def finish(i):
            src = lax.rem(me - i + seq, seq)
            maybe(src < owners, owners == seq, lambda: arrival(i).wait_recv())

        def sent(i):
            peer = lax.rem(me + i, seq)
            maybe(me < owners, owners == seq, lambda: copy(i, peer).wait_send())

        return start, finish, sent

    def sums(decay):
        span = decay.shape[1]
        later = ones_where(iota((span, span), 0) >= iota((span, span), 1))
        earlier = ones_where(iota((span, span), 0) <= iota((span, span), 1))
        heads = ones_where(iota((width, MIXER_STREAMS), 0) // HEAD_DIM == iota((width, MIXER_STREAMS), 1))
        wide = jnp.zeros((span, width), F32)
        flat = jnp.zeros((MIXER_STREAMS, span), F32)
        for piece_of in split3(decay):
            wide = wide + dot_nt(later, dot(heads, piece_of).astype(BF16))
            flat = flat + dot(piece_of, earlier)
        return wide, flat

    def summarise(joined, wide, layer):
        span = joined.shape[0]
        total = wide[span - 1 : span, :]
        keys = (joined[:, width : 2 * width].astype(F32) * jnp.exp(total - wide)).astype(BF16)
        values = joined[:, 2 * width :]
        first_head = iota((HEAD_DIM, LANES), 1) < HEAD_DIM
        tail_row = iota((16, LANES), 0)
        for g in range(groups):
            cols = slice(g * LANES, (g + 1) * LANES)
            state = dot_tn(keys[:, cols], values[:, cols])
            packed = jnp.where(first_head, state[:HEAD_DIM], state[HEAD_DIM:]).astype(BF16)
            hi, mid, low = (jnp.broadcast_to(t.astype(F32), (16, LANES)) for t in split3(total[:, cols]))
            tail = jnp.where(tail_row == 0, hi, jnp.where(tail_row == 1, mid, jnp.where(tail_row == 2, low, 0.0)))
            tail = tail.astype(BF16)
            for r in range(per_group):
                o = g * per_group + r
                a_send[layer, o, :state_rows] = packed[r * state_rows : (r + 1) * state_rows]
                a_send[layer, o, state_rows:] = tail

    def own_summary(layer):
        maybe(me < owners, owners == seq, lambda: store(a_recv, layer, me, a_send[layer, me]))

    def store(ref, layer, index, value):
        ref[layer, index] = value

    def prefix(layer):
        def step(j, before):
            b_send[layer, j] = before.astype(BF16)
            message = a_recv[layer, j].astype(F32)
            total = message[state_rows : state_rows + 1] + message[state_rows + 1 : state_rows + 2]
            total = total + message[state_rows + 2 : state_rows + 3]
            return before * jnp.exp(total) + message[:state_rows]

        def run():
            before = jnp.zeros((state_rows, LANES), F32)
            if seq <= UNROLL:
                for j in range(seq):
                    before = step(j, before)
            else:
                lax.fori_loop(0, seq, step, before)
            b_recv[layer, me] = b_send[layer, me]

        maybe(me < owners, owners == seq, run)

    def inner(joined, wide, flat, num, g):
        span = joined.shape[0]
        cols = slice(g * LANES, (g + 1) * LANES)
        query = joined[:, cols]
        key = joined[:, width + g * LANES : width + (g + 1) * LANES]
        value = joined[:, 2 * width + g * LANES : 2 * width + (g + 1) * LANES]
        causal = iota((span, span), 0) >= iota((span, span), 1)
        total = jnp.zeros((span, LANES), F32)
        for a in range(2):
            mask = ones_where(iota((1, LANES), 1) // HEAD_DIM == a)
            h = 2 * g + a
            gap = wide[:, h * HEAD_DIM : h * HEAD_DIM + 1] - flat[h : h + 1, :]
            weight = jnp.exp(jnp.where(causal, gap, -1e30))
            scores = dot_nt(query, key * mask)
            total = total + dot((scores * weight).astype(BF16), value * mask)
        num[:, cols] = total

    def finish_heads(joined, wide, num, att, layer):
        same = ones_where(iota((LANES, LANES), 0) // HEAD_DIM == iota((LANES, LANES), 1) // HEAD_DIM)
        for g in range(groups):
            cols = slice(g * LANES, (g + 1) * LANES)
            packed = jnp.concatenate(
                [b_recv[layer, g * per_group + r] for r in range(per_group)], axis=0
            )
            entering = jnp.concatenate([packed, packed], axis=0) * same
            total = num[:, cols] + dot(joined[:, cols], entering) * jnp.exp(wide[:, cols])
            mean = dot((total * total).astype(BF16), same) * (1.0 / HEAD_DIM)
            att[:, cols] = (total * lax.rsqrt(mean + EPS)).astype(BF16)

    x = points[...].astype(F32)
    loads[0].wait()
    project(x, wq1, joined_one)
    wide, flat = sums(decay_one[...])
    summarise(joined_one, wide, 0)
    start, finish, sent_a1 = to_owners(0, 0)
    loop(1, seq, start)
    own_summary(0)
    many = half > UNROLL // 2
    pumps = iter(()) if many else iter(range(1, half + 1))

    def pump():
        k = next(pumps, None)
        if k is not None:
            relay_step(k)

    pump()
    for g in range(groups):
        inner(joined_one, wide, flat, num_one, g)
    loop(1, seq, finish)
    prefix(0)
    start, finish, sent_b1 = from_owners(1, 0)
    loop(1, seq, start)
    pump()

    blocks = target.shape[1]
    shift_cap, shift_row = log2(CAP), log2(BR)
    local_blocks = rows // BR
    shift_local = log2(local_blocks)
    slot = target[...]
    device_of = jnp.broadcast_to(lax.shift_right_logical(slot, shift_cap).astype(F32), (8, blocks)).astype(BF16)
    slot_in = lax.bitwise_and(slot, CAP - 1)
    token_block = iota((rows, blocks), 0) // BR + me * local_blocks
    pick = ones_where(token_block == iota((rows, blocks), 1))
    to_row = dot_nt(device_of, pick)[0:1]
    to_col = dot_nt(pick, device_of)[:, 0:1]
    t0, t1 = iota((rows, rows), 0), iota((rows, rows), 1)
    before = (t0 // BR < t1 // BR) & (t0 % BR == 0) & (to_row == to_col)
    rank = jnp.sum(jnp.where(before, 1.0, 0.0), axis=0, keepdims=True)
    send_row = to_row * pair_rows + rank * BR + (iota((1, rows), 1) % BR).astype(F32)
    all_rows = seq * pair_rows
    scatter = ones_where(iota((all_rows, rows), 0).astype(F32) == send_row)

    here = lax.shift_right_logical(slot, shift_cap) == me
    here_rows = ones_where(jnp.broadcast_to(here, (8, blocks)))
    chunk = min(LANES, blocks)
    c0, c1 = iota((chunk, chunk), 0), iota((chunk, chunk), 1)
    lower = ones_where((c0 // local_blocks == c1 // local_blocks) & (c1 < c0))
    same_index = ones_where(c0 == c1)
    placing = jnp.zeros((rows_two, all_rows), F32)
    used = jnp.zeros((8, rows_two), F32)
    row_slot = iota((rows_two, chunk), 0) // BR
    in_row = iota((chunk, all_rows), 1) // BR * BR
    for c in range(blocks // chunk):
        cols = slice(c * chunk, (c + 1) * chunk)
        rank_col = dot_nt(lower, here_rows[:, cols])[:, 0:1]
        here_col = dot_nt(same_index, here_rows[:, cols])[:, 0:1]
        block_col = (iota((chunk, 1), 0) + c * chunk) // local_blocks
        base = block_col.astype(F32) * pair_rows + rank_col * BR
        base = jnp.where(here_col > 0.5, base, -1.0)
        taken = ones_where((row_slot == slot_in[:, cols]) & here[:, cols])
        placing = placing + dot(taken, ones_where(base == in_row.astype(F32)))
        used = used + dot_nt(jnp.ones((8, chunk), BF16), taken)
    sub = iota((rows_two, all_rows), 0) % BR == iota((rows_two, all_rows), 1) % BR
    gather = jnp.where(sub, placing, 0.0).astype(BF16)
    wide_two, flat_two = sums(decay_two[...] * used[0:1])

    loop(1, seq, finish)
    finish_heads(joined_one, wide, num_one, att_one, 0)
    loads[1].wait()
    first = (x + dot(att_one[...], wo1[...])).astype(BF16)
    normed = rms(first.astype(F32)).astype(BF16)

    def feed(s):
        hidden = gelu(dot(normed, up[s])).astype(BF16)
        acc[...] += dot(hidden, down[s])

    acc[...] = first.astype(F32)
    pump()
    for copy in own:
        copy.wait()
    feed(me)

    def take(k):
        if halves == 2:
            for way, w in routes(k):
                core(way, w, k).wait_recv()
        feed(origin(0, k))
        if not (isinstance(k, int) and k == half):
            feed(origin(1, k))

    if many:
        loop(1, half - 1, lambda k: relay(k, both, both))
        relay(half - 1, both, last)
        relay(half, last, [])
        loop(1, half, take)
        take(half)
    else:
        for k in range(1, half + 1):
            take(k)
            pump()

    layer_out = acc[...].astype(BF16)
    chosen = dot(scatter, layer_out).astype(BF16)
    for j in range(seq):
        blk_send[j] = chosen[j * pair_rows : (j + 1) * pair_rows]
    move, moved = exchange(2, blk_send, blk_recv, seq)
    loop(1, seq, lambda i: move(i, lax.rem(me + i, seq)).start())
    blk_recv[me] = blk_send[me]
    loads[2].wait()
    loop(1, seq, lambda i: moved(i).wait_recv())
    placed = dot(gather, blk_recv[...].reshape(all_rows, width))

    project(placed, wq2, joined_two)
    summarise(joined_two, wide_two, 1)
    start, finish, sent_a2 = to_owners(3, 1)
    loop(1, seq, start)
    own_summary(1)
    for g in range(groups // 2):
        inner(joined_two, wide_two, flat_two, num_two, g)
    loop(1, seq, finish)
    prefix(1)
    start, finish, sent_b2 = from_owners(4, 1)
    loop(1, seq, start)
    for g in range(groups // 2, groups):
        inner(joined_two, wide_two, flat_two, num_two, g)
    loads[3].wait()
    loop(1, seq, finish)
    finish_heads(joined_two, wide_two, num_two, att_two, 1)
    out[...] = (placed + dot(att_two[...], wo2[...])).astype(BF16)

    for sent in (sent_a1, sent_b1, sent_a2, sent_b2):
        loop(1, seq, sent)
    loop(1, seq, lambda i: move(i, lax.rem(me + i, seq)).wait_send())
    for way, w in routes(1):
        ring(way, w, 1, first=True).wait_send()

    def relayed(k):
        for way, w in routes(k):
            if not (isinstance(k, int) and k == 1):
                ring(way, w, k).wait_send()
            if halves == 2:
                core(way, w, k).wait_send()

    relayed(1)
    loop(2, half, relayed)
    relayed(half)


def shards(seq, reps, points, decay_one, decay_two, block_target, w_qkv_one, w_out_one, w_up, w_down, w_qkv_two, w_out_two):
    rows, width = points.shape
    rows_two = CAP * BR
    groups = width // LANES
    owners = min(seq, 4 * groups)
    state_rows = HEAD_DIM * groups // owners
    pair_rows = max(16, max(1, CAP // seq) * BR)
    half = seq // 2
    hidden = w_up.shape[1]
    vmem = pl.BlockSpec(memory_space=pltpu.VMEM)
    anywhere = pl.BlockSpec(memory_space=pl.ANY)
    dma = pltpu.SemaphoreType.DMA
    return pl.pallas_call(
        functools.partial(kernel, seq, reps, owners),
        out_shape=jax.ShapeDtypeStruct((rows_two, width), BF16),
        in_specs=[vmem] * 4 + [anywhere] * 6,
        out_specs=vmem,
        scratch_shapes=[
            pltpu.VMEM(w_qkv_one.shape, BF16),
            pltpu.VMEM(w_out_one.shape, BF16),
            pltpu.VMEM(w_qkv_two.shape, BF16),
            pltpu.VMEM(w_out_two.shape, BF16),
            pltpu.VMEM((seq, width, hidden), BF16),
            pltpu.VMEM((seq, hidden, width), BF16),
            pltpu.VMEM((rows, 3 * width), BF16),
            pltpu.VMEM((rows_two, 3 * width), BF16),
            pltpu.VMEM((rows, width), F32),
            pltpu.VMEM((rows_two, width), F32),
            pltpu.VMEM((rows, width), BF16),
            pltpu.VMEM((rows_two, width), BF16),
            pltpu.VMEM((2, owners, state_rows + 16, LANES), BF16),
            pltpu.VMEM((2, seq, state_rows + 16, LANES), BF16),
            pltpu.VMEM((2, seq, state_rows, LANES), BF16),
            pltpu.VMEM((2, owners, state_rows, LANES), BF16),
            pltpu.VMEM((seq, pair_rows, width), BF16),
            pltpu.VMEM((seq, pair_rows, width), BF16),
            pltpu.VMEM((rows, width), F32),
            dma((4,)),
            dma((2,)),
            dma((2, 2, half)),
            dma((2, 2, half)),
            dma((2, 2, half)),
            dma((2, 2, half)),
            dma((5, seq)),
            dma((5, seq)),
        ],
        compiler_params=pltpu.CompilerParams(
            collective_id=0, has_side_effects=True, vmem_limit_bytes=56 * 1024 * 1024
        ),
    )(
        points, decay_one, decay_two, block_target.reshape(1, -1),
        w_qkv_one, w_out_one, w_up, w_down, w_qkv_two, w_out_two,
    )


def solution(mesh):
    in_specs = (
        P(("rep", "seq"), None),
        P(None, ("rep", "seq")),
        P(None, ("rep", "seq")),
        P("rep"),
        P(),
        P(),
        P(None, "seq"),
        P("seq", None),
        P(),
        P(),
    )
    out_specs = P(("rep", "seq"), None)
    body = functools.partial(shards, mesh.shape["seq"], mesh.shape["rep"])
    return jax.shard_map(body, mesh=mesh, in_specs=in_specs, out_specs=out_specs, check_vma=False)
```

```python
import functools

import jax
import jax.numpy as jnp
from jax import lax
from jax.experimental import pallas as pl
from jax.experimental.pallas import tpu as pltpu
from jax.sharding import PartitionSpec as P

MIXER_STREAMS = 8
HEAD_DIM = 64
BR = 8
CAP = 32
LANES = 128
EPS = 1e-05
F32 = jnp.float32
BF16 = jnp.bfloat16
MESH = pl.DeviceIdType.MESH
UNROLL = 16


def dot(a, b):
    return jnp.dot(a, b, preferred_element_type=F32)


def dot_nt(a, b):
    return lax.dot_general(a, b, (((1,), (1,)), ((), ())), preferred_element_type=F32)


def dot_tn(a, b):
    return lax.dot_general(a, b, (((0,), (0,)), ((), ())), preferred_element_type=F32)


def iota(shape, dim):
    return lax.broadcasted_iota(jnp.int32, shape, dim)


def ones_where(mask):
    return jnp.where(mask, 1.0, 0.0).astype(BF16)


def split3(x):
    hi = x.astype(BF16)
    rest = x - hi.astype(F32)
    mid = rest.astype(BF16)
    low = (rest - mid.astype(F32)).astype(BF16)
    return hi, mid, low


def rms(x):
    return x * lax.rsqrt(jnp.mean(x * x, axis=-1, keepdims=True) + EPS)


def gelu(x):
    return 0.5 * x * (1.0 + jnp.tanh(0.7978845608028654 * (x + 0.044715 * (x * x * x))))


def loop(start, stop, body):
    if stop - start <= UNROLL:
        for i in range(start, stop):
            body(i)
    else:
        def step(i, carry):
            body(i)
            return carry

        lax.fori_loop(start, stop, step, 0)


def log2(n):
    assert n & (n - 1) == 0
    return n.bit_length() - 1


def project(normed, weight, joined):
    width = normed.shape[1]
    joined[:, :width] = (dot(normed, weight[:, :width]) * HEAD_DIM**-0.5).astype(BF16)
    joined[:, width:] = dot(normed, weight[:, width:]).astype(BF16)


def sums(decay, width):
    span = decay.shape[1]
    later = ones_where(iota((span, span), 0) >= iota((span, span), 1))
    earlier = ones_where(iota((span, span), 0) <= iota((span, span), 1))
    heads = ones_where(iota((width, MIXER_STREAMS), 0) // HEAD_DIM == iota((width, MIXER_STREAMS), 1))
    wide = jnp.zeros((span, width), F32)
    flat = jnp.zeros((MIXER_STREAMS, span), F32)
    for piece_of in split3(decay):
        wide = wide + dot_nt(later, dot(heads, piece_of).astype(BF16))
        flat = flat + dot(piece_of, earlier)
    return wide, flat


def kernel(
    seq, reps, owners,
    points, decay_one, decay_two, target, w_qkv_one, w_out_one, w_up, w_down, w_qkv_two, w_out_two,
    out,
    wq1, wo1, wq2, wo2, up, down,
    joined_one, joined_two, num_one, num_two, att_one, att_two,
    a_send, a_recv, b_send, b_recv, blk_send, blk_recv, acc,
    load_sem, own_sem, ring_send, ring_recv, core_send, core_recv, side_send, side_recv, pass_send, pass_recv,
    ex_send, ex_recv,
):
    me = lax.axis_index("seq")
    rep = lax.axis_index("rep")
    rows, width = points.shape
    rows_two = out.shape[0]
    half = seq // 2
    halves = 2 if reps % 2 == 0 else 1
    part = width // halves
    mine = rep % halves
    partner = rep + 1 - 2 * (rep % 2)
    quarters = 4 if reps % 4 == 0 else halves
    fine = width // quarters
    across = rep + 2 - 4 * ((rep // 2) % 2)
    crossing = quarters == 4
    neighbours = [partner] * (halves == 2) + [across] * crossing
    groups = width // LANES
    per_group = owners // groups
    state_rows = HEAD_DIM // per_group
    pair_rows = blk_send.shape[1]

    loads = [
        pltpu.make_async_copy(src, dst, load_sem.at[i])
        for i, (src, dst) in enumerate(
            ((w_qkv_one, wq1), (w_out_one, wo1), (w_qkv_two, wq2), (w_out_two, wo2))
        )
    ]
    loads[0].start()
    own = [
        pltpu.make_async_copy(w_up, up.at[me], own_sem.at[0]),
        pltpu.make_async_copy(w_down, down.at[me], own_sem.at[1]),
    ]

    barrier = pltpu.get_barrier_semaphore()

    def greet(i):
        pl.semaphore_signal(
            barrier, inc=1, device_id={"seq": lax.rem(me + i, seq)}, device_id_type=MESH
        )

    loop(1, seq, greet)
    for other in neighbours:
        pl.semaphore_signal(barrier, inc=1, device_id={"rep": other}, device_id_type=MESH)
    x = points[...].astype(F32)
    normed_one = rms(x).astype(BF16)
    wide, flat = sums(decay_one[...], width)
    pl.semaphore_wait(barrier, seq - 1 + len(neighbours))

    place = jnp.where(me % 2 == 0, me // 2, seq - 1 - me // 2)

    def at_place(p):
        q = lax.rem(p + 2 * seq, seq)
        return jnp.where(q < half, 2 * q, 2 * (seq - 1 - q) + 1)

    neighbour = (at_place(place + 1), at_place(place - 1))

    quarter = (rep % 2) * (quarters // 2) + (rep // 2) % 2 if crossing else mine

    def up_piece(s, index):
        return up.at[s, pl.ds(pl.multiple_of(index * fine, fine), fine), :]

    def piece(w, s):
        if w == 0:
            return up_piece(s, quarter)
        return down.at[s, :, pl.ds(pl.multiple_of(mine * part, part), part)]

    def own_piece(w):
        if w == 0:
            return w_up.at[pl.ds(pl.multiple_of(quarter * fine, fine), fine), :]
        return w_down.at[:, pl.ds(pl.multiple_of(mine * part, part), part)]

    def origin(way, k):
        return at_place(place - k if way == 0 else place + k)

    def ring(way, w, k, first=False):
        where = piece(w, me if first else origin(way, k - 1))
        return pltpu.make_async_remote_copy(
            src_ref=own_piece(w) if first else where,
            dst_ref=where,
            send_sem=ring_send.at[way, w, k - 1],
            recv_sem=ring_recv.at[way, w, k - 1],
            device_id={"seq": neighbour[way]},
            device_id_type=MESH,
        )

    def ring_arrival(way, w, k):
        where = piece(w, origin(way, k))
        return pltpu.make_async_remote_copy(
            src_ref=where,
            dst_ref=where,
            send_sem=ring_send.at[way, w, k - 1],
            recv_sem=ring_recv.at[way, w, k - 1],
            device_id={"seq": neighbour[way]},
            device_id_type=MESH,
        )

    def core(way, w, k):
        where = piece(w, origin(way, k))
        return pltpu.make_async_remote_copy(
            src_ref=where,
            dst_ref=where,
            send_sem=core_send.at[way, w, k - 1],
            recv_sem=core_recv.at[way, w, k - 1],
            device_id={"rep": partner},
            device_id_type=MESH,
        )

    def side(way, k):
        where = up_piece(origin(way, k), quarter)
        return pltpu.make_async_remote_copy(
            src_ref=where,
            dst_ref=where,
            send_sem=side_send.at[way, k - 1],
            recv_sem=side_recv.at[way, k - 1],
            device_id={"rep": across},
            device_id_type=MESH,
        )

    def side_arrival(way, k):
        where = up_piece(origin(way, k), quarter + 1 - 2 * (quarter % 2))
        return pltpu.make_async_remote_copy(
            src_ref=where,
            dst_ref=where,
            send_sem=side_send.at[way, k - 1],
            recv_sem=side_recv.at[way, k - 1],
            device_id={"rep": across},
            device_id_type=MESH,
        )

    def hand_on(way, k):
        where = up_piece(origin(way, k), quarter + 1 - 2 * (quarter % 2))
        return pltpu.make_async_remote_copy(
            src_ref=where,
            dst_ref=where,
            send_sem=pass_send.at[way, k - 1],
            recv_sem=pass_recv.at[way, k - 1],
            device_id={"rep": partner},
            device_id_type=MESH,
        )

    both = [(way, w) for w in range(2) for way in range(2)]
    last = [(0, 0), (1, 1)]

    def routes(k):
        return last if isinstance(k, int) and k == half else both

    def relay(k, routes_now, routes_next):
        for way, w in routes_now:
            ring_arrival(way, w, k).wait_recv()
            if (way, w) in routes_next:
                ring(way, w, k + 1).start()
            if crossing and w == 0:
                side(way, k).start()
            if halves == 2:
                core(way, w, k).start()

    def relay_part(k, w):
        relay(
            k,
            [route for route in routes(k) if route[1] == w],
            routes(k + 1) if k < half else [],
        )

    def crossed(k):
        if crossing:
            for way, w in routes(k):
                if w == 0:
                    side_arrival(way, k).wait_recv()
                    hand_on(way, k).start()

    for way, w in routes(1):
        ring(way, w, 1, first=True).start()
    for copy in loads[1:] + own:
        copy.start()

    def exchange(index, source, target_buf, count):
        def copy(i, peer):
            return pltpu.make_async_remote_copy(
                src_ref=source.at[peer],
                dst_ref=target_buf.at[me],
                send_sem=ex_send.at[index, i],
                recv_sem=ex_recv.at[index, i],
                device_id={"seq": peer},
                device_id_type=MESH,
            )

        def arrival(i):
            src = lax.rem(me - i + seq, seq)
            return pltpu.make_async_remote_copy(
                src_ref=target_buf.at[src],
                dst_ref=target_buf.at[src],
                send_sem=ex_send.at[index, i],
                recv_sem=ex_recv.at[index, i],
                device_id={"seq": lax.rem(me + i, seq)},
                device_id_type=MESH,
            )

        return copy, arrival

    def maybe(cond, all_true, body):
        if all_true:
            body()
        else:
            pl.when(cond)(body)

    def to_owners(index, layer):
        copy, arrival = exchange(index, a_send.at[layer], a_recv.at[layer], owners)

        def start(i):
            peer = lax.rem(me + i, seq)
            maybe(peer < owners, owners == seq, lambda: copy(i, peer).start())

        def finish(i):
            peer = lax.rem(me + i, seq)
            maybe(me < owners, owners == seq, lambda: arrival(i).wait_recv())

        def sent(i):
            peer = lax.rem(me + i, seq)
            maybe(peer < owners, owners == seq, lambda: copy(i, peer).wait_send())

        return start, finish, sent

    def from_owners(index, layer):
        copy, arrival = exchange(index, b_send.at[layer], b_recv.at[layer], seq)

        def start(i):
            peer = lax.rem(me + i, seq)
            maybe(me < owners, owners == seq, lambda: copy(i, peer).start())

        def finish(i):
            src = lax.rem(me - i + seq, seq)
            maybe(src < owners, owners == seq, lambda: arrival(i).wait_recv())

        def sent(i):
            peer = lax.rem(me + i, seq)
            maybe(me < owners, owners == seq, lambda: copy(i, peer).wait_send())

        return start, finish, sent

    def summarise(joined, wide, layer):
        span = joined.shape[0]
        total = wide[span - 1 : span, :]
        keys = (joined[:, width : 2 * width].astype(F32) * jnp.exp(total - wide)).astype(BF16)
        values = joined[:, 2 * width :]
        first_head = iota((HEAD_DIM, LANES), 1) < HEAD_DIM
        tail_row = iota((16, LANES), 0)
        for g in range(groups):
            cols = slice(g * LANES, (g + 1) * LANES)
            state = dot_tn(keys[:, cols], values[:, cols])
            packed = jnp.where(first_head, state[:HEAD_DIM], state[HEAD_DIM:]).astype(BF16)
            hi, mid, low = (jnp.broadcast_to(t.astype(F32), (16, LANES)) for t in split3(total[:, cols]))
            tail = jnp.where(tail_row == 0, hi, jnp.where(tail_row == 1, mid, jnp.where(tail_row == 2, low, 0.0)))
            tail = tail.astype(BF16)
            for r in range(per_group):
                o = g * per_group + r
                a_send[layer, o, :state_rows] = packed[r * state_rows : (r + 1) * state_rows]
                a_send[layer, o, state_rows:] = tail

    def own_summary(layer):
        maybe(me < owners, owners == seq, lambda: store(a_recv, layer, me, a_send[layer, me]))

    def store(ref, layer, index, value):
        ref[layer, index] = value

    def prefix(layer):
        def step(j, before):
            b_send[layer, j] = before.astype(BF16)
            message = a_recv[layer, j].astype(F32)
            total = message[state_rows : state_rows + 1] + message[state_rows + 1 : state_rows + 2]
            total = total + message[state_rows + 2 : state_rows + 3]
            return before * jnp.exp(total) + message[:state_rows]

        def run():
            before = jnp.zeros((state_rows, LANES), F32)
            if seq <= UNROLL:
                for j in range(seq):
                    before = step(j, before)
            else:
                lax.fori_loop(0, seq, step, before)
            b_recv[layer, me] = b_send[layer, me]

        maybe(me < owners, owners == seq, run)

    def inner(joined, wide, flat, num, g):
        span = joined.shape[0]
        cols = slice(g * LANES, (g + 1) * LANES)
        query = joined[:, cols]
        key = joined[:, width + g * LANES : width + (g + 1) * LANES]
        value = joined[:, 2 * width + g * LANES : 2 * width + (g + 1) * LANES]
        causal = iota((span, span), 0) >= iota((span, span), 1)
        total = jnp.zeros((span, LANES), F32)
        for a in range(2):
            mask = ones_where(iota((1, LANES), 1) // HEAD_DIM == a)
            h = 2 * g + a
            gap = wide[:, h * HEAD_DIM : h * HEAD_DIM + 1] - flat[h : h + 1, :]
            weight = jnp.exp(jnp.where(causal, gap, -1e30))
            scores = dot_nt(query, key * mask)
            total = total + dot((scores * weight).astype(BF16), value * mask)
        num[:, cols] = total

    def finish_heads(joined, wide, num, att, layer):
        same = ones_where(iota((LANES, LANES), 0) // HEAD_DIM == iota((LANES, LANES), 1) // HEAD_DIM)
        for g in range(groups):
            cols = slice(g * LANES, (g + 1) * LANES)
            packed = jnp.concatenate(
                [b_recv[layer, g * per_group + r] for r in range(per_group)], axis=0
            )
            entering = jnp.concatenate([packed, packed], axis=0) * same
            total = num[:, cols] + dot(joined[:, cols], entering) * jnp.exp(wide[:, cols])
            mean = dot((total * total).astype(BF16), same) * (1.0 / HEAD_DIM)
            att[:, cols] = (total * lax.rsqrt(mean + EPS)).astype(BF16)

    loads[0].wait()
    project(normed_one, wq1, joined_one)
    summarise(joined_one, wide, 0)
    start, finish, sent_a1 = to_owners(0, 0)
    loop(1, seq, start)
    own_summary(0)
    many = half > UNROLL // 2
    pumps = [] if many else [(k, w) for k in range(1, half + 1) for w in range(2)]

    def pump(count=1):
        for _ in range(min(count, len(pumps))):
            k, w = pumps.pop(0)
            relay_part(k, w)
            if w == 1:
                crossed(k)

    pump(2)
    for g in range(groups):
        inner(joined_one, wide, flat, num_one, g)
    loop(1, seq, finish)
    prefix(0)
    start, finish, sent_b1 = from_owners(1, 0)
    loop(1, seq, start)
    pump()

    blocks = target.shape[1]
    shift_cap, shift_row = log2(CAP), log2(BR)
    local_blocks = rows // BR
    shift_local = log2(local_blocks)
    slot = target[...]
    device_of = jnp.broadcast_to(lax.shift_right_logical(slot, shift_cap).astype(F32), (8, blocks)).astype(BF16)
    slot_in = lax.bitwise_and(slot, CAP - 1)
    token_block = iota((rows, blocks), 0) // BR + me * local_blocks
    pick = ones_where(token_block == iota((rows, blocks), 1))
    to_row = dot_nt(device_of, pick)[0:1]
    to_col = dot_nt(pick, device_of)[:, 0:1]
    t0, t1 = iota((rows, rows), 0), iota((rows, rows), 1)
    before = (t0 // BR < t1 // BR) & (t0 % BR == 0) & (to_row == to_col)
    rank = jnp.sum(jnp.where(before, 1.0, 0.0), axis=0, keepdims=True)
    send_row = to_row * pair_rows + rank * BR + (iota((1, rows), 1) % BR).astype(F32)
    all_rows = seq * pair_rows
    scatter = ones_where(iota((all_rows, rows), 0).astype(F32) == send_row)

    here = lax.shift_right_logical(slot, shift_cap) == me
    here_rows = ones_where(jnp.broadcast_to(here, (8, blocks)))
    chunk = min(LANES, blocks)
    c0, c1 = iota((chunk, chunk), 0), iota((chunk, chunk), 1)
    lower = ones_where((c0 // local_blocks == c1 // local_blocks) & (c1 < c0))
    same_index = ones_where(c0 == c1)
    placing = jnp.zeros((rows_two, all_rows), F32)
    used = jnp.zeros((8, rows_two), F32)
    row_slot = iota((rows_two, chunk), 0) // BR
    in_row = iota((chunk, all_rows), 1) // BR * BR
    for c in range(blocks // chunk):
        cols = slice(c * chunk, (c + 1) * chunk)
        rank_col = dot_nt(lower, here_rows[:, cols])[:, 0:1]
        here_col = dot_nt(same_index, here_rows[:, cols])[:, 0:1]
        block_col = (iota((chunk, 1), 0) + c * chunk) // local_blocks
        base = block_col.astype(F32) * pair_rows + rank_col * BR
        base = jnp.where(here_col > 0.5, base, -1.0)
        taken = ones_where((row_slot == slot_in[:, cols]) & here[:, cols])
        placing = placing + dot(taken, ones_where(base == in_row.astype(F32)))
        used = used + dot_nt(jnp.ones((8, chunk), BF16), taken)
    sub = iota((rows_two, all_rows), 0) % BR == iota((rows_two, all_rows), 1) % BR
    gather = jnp.where(sub, placing, 0.0).astype(BF16)
    wide_two, flat_two = sums(decay_two[...] * used[0:1], width)
    pump()

    loop(1, seq, finish)
    finish_heads(joined_one, wide, num_one, att_one, 0)
    loads[1].wait()
    first = (x + dot(att_one[...], wo1[...])).astype(BF16)
    normed = rms(first.astype(F32)).astype(BF16)

    def feed(s):
        hidden = gelu(dot(normed, up[s])).astype(BF16)
        acc[...] += dot(hidden, down[s])

    acc[...] = first.astype(F32)
    pump()
    for copy in own:
        copy.wait()
    feed(me)

    def take(k):
        if crossing:
            for way, w in routes(k):
                if w == 0:
                    hand_on(way, k).wait_recv()
        if halves == 2:
            for way, w in routes(k):
                core(way, w, k).wait_recv()
        feed(origin(0, k))
        if not (isinstance(k, int) and k == half):
            feed(origin(1, k))

    if many:
        loop(1, half - 1, lambda k: relay(k, both, both))
        relay(half - 1, both, last)
        relay(half, last, [])
        loop(1, half, crossed)
        crossed(half)
        loop(1, half, take)
        take(half)
    else:
        for k in range(1, half + 1):
            take(k)
            pump(1 if k == 1 else 2)
        assert not pumps

    layer_out = acc[...].astype(BF16)
    chosen = dot(scatter, layer_out).astype(BF16)
    for j in range(seq):
        blk_send[j] = chosen[j * pair_rows : (j + 1) * pair_rows]
    move, moved = exchange(2, blk_send, blk_recv, seq)
    loop(1, seq, lambda i: move(i, lax.rem(me + i, seq)).start())
    blk_recv[me] = blk_send[me]
    loads[2].wait()
    loop(1, seq, lambda i: moved(i).wait_recv())
    placed = dot(gather, blk_recv[...].reshape(all_rows, width))

    project(rms(placed).astype(BF16), wq2, joined_two)
    summarise(joined_two, wide_two, 1)
    start, finish, sent_a2 = to_owners(3, 1)
    loop(1, seq, start)
    own_summary(1)
    for g in range(groups // 2):
        inner(joined_two, wide_two, flat_two, num_two, g)
    loop(1, seq, finish)
    prefix(1)
    start, finish, sent_b2 = from_owners(4, 1)
    loop(1, seq, start)
    for g in range(groups // 2, groups):
        inner(joined_two, wide_two, flat_two, num_two, g)
    loads[3].wait()
    loop(1, seq, finish)
    finish_heads(joined_two, wide_two, num_two, att_two, 1)
    out[...] = (placed + dot(att_two[...], wo2[...])).astype(BF16)

    for sent in (sent_a1, sent_b1, sent_a2, sent_b2):
        loop(1, seq, sent)
    loop(1, seq, lambda i: move(i, lax.rem(me + i, seq)).wait_send())
    for way, w in routes(1):
        ring(way, w, 1, first=True).wait_send()

    def relayed(k):
        for way, w in routes(k):
            if not (isinstance(k, int) and k == 1):
                ring(way, w, k).wait_send()
            if halves == 2:
                core(way, w, k).wait_send()
            if crossing and w == 0:
                side(way, k).wait_send()
                hand_on(way, k).wait_send()

    relayed(1)
    loop(2, half, relayed)
    relayed(half)


def shards(seq, reps, points, decay_one, decay_two, block_target, w_qkv_one, w_out_one, w_up, w_down, w_qkv_two, w_out_two):
    rows, width = points.shape
    rows_two = CAP * BR
    groups = width // LANES
    owners = min(seq, 4 * groups)
    state_rows = HEAD_DIM * groups // owners
    pair_rows = max(16, max(1, CAP // seq) * BR)
    half = seq // 2
    hidden = w_up.shape[1]
    vmem = pl.BlockSpec(memory_space=pltpu.VMEM)
    anywhere = pl.BlockSpec(memory_space=pl.ANY)
    dma = pltpu.SemaphoreType.DMA
    return pl.pallas_call(
        functools.partial(kernel, seq, reps, owners),
        out_shape=jax.ShapeDtypeStruct((rows_two, width), BF16),
        in_specs=[vmem] * 4 + [anywhere] * 6,
        out_specs=vmem,
        scratch_shapes=[
            pltpu.VMEM(w_qkv_one.shape, BF16),
            pltpu.VMEM(w_out_one.shape, BF16),
            pltpu.VMEM(w_qkv_two.shape, BF16),
            pltpu.VMEM(w_out_two.shape, BF16),
            pltpu.VMEM((seq, width, hidden), BF16),
            pltpu.VMEM((seq, hidden, width), BF16),
            pltpu.VMEM((rows, 3 * width), BF16),
            pltpu.VMEM((rows_two, 3 * width), BF16),
            pltpu.VMEM((rows, width), F32),
            pltpu.VMEM((rows_two, width), F32),
            pltpu.VMEM((rows, width), BF16),
            pltpu.VMEM((rows_two, width), BF16),
            pltpu.VMEM((2, owners, state_rows + 16, LANES), BF16),
            pltpu.VMEM((2, seq, state_rows + 16, LANES), BF16),
            pltpu.VMEM((2, seq, state_rows, LANES), BF16),
            pltpu.VMEM((2, owners, state_rows, LANES), BF16),
            pltpu.VMEM((seq, pair_rows, width), BF16),
            pltpu.VMEM((seq, pair_rows, width), BF16),
            pltpu.VMEM((rows, width), F32),
            dma((4,)),
            dma((2,)),
            dma((2, 2, half)),
            dma((2, 2, half)),
            dma((2, 2, half)),
            dma((2, 2, half)),
            dma((2, half)),
            dma((2, half)),
            dma((2, half)),
            dma((2, half)),
            dma((5, seq)),
            dma((5, seq)),
        ],
        compiler_params=pltpu.CompilerParams(
            collective_id=0, has_side_effects=True, vmem_limit_bytes=56 * 1024 * 1024
        ),
    )(
        points, decay_one, decay_two, block_target.reshape(1, -1),
        w_qkv_one, w_out_one, w_up, w_down, w_qkv_two, w_out_two,
    )


def solution(mesh):
    in_specs = (
        P(("rep", "seq"), None),
        P(None, ("rep", "seq")),
        P(None, ("rep", "seq")),
        P("rep"),
        P(),
        P(),
        P(None, "seq"),
        P("seq", None),
        P(),
        P(),
    )
    out_specs = P(("rep", "seq"), None)
    body = functools.partial(shards, mesh.shape["seq"], mesh.shape["rep"])
    return jax.shard_map(body, mesh=mesh, in_specs=in_specs, out_specs=out_specs, check_vma=False)
```

```python
import functools

import jax
import jax.numpy as jnp
from jax import lax
from jax.experimental import pallas as pl
from jax.experimental.pallas import tpu as pltpu
from jax.sharding import PartitionSpec as P

MIXER_STREAMS = 8
HEAD_DIM = 64
BR = 8
CAP = 32
LANES = 128
EPS = 1e-05
F32 = jnp.float32
BF16 = jnp.bfloat16
MESH = pl.DeviceIdType.MESH
UNROLL = 16


def dot(a, b):
    return jnp.dot(a, b, preferred_element_type=F32)


def dot_nt(a, b):
    return lax.dot_general(a, b, (((1,), (1,)), ((), ())), preferred_element_type=F32)


def dot_tn(a, b):
    return lax.dot_general(a, b, (((0,), (0,)), ((), ())), preferred_element_type=F32)


def iota(shape, dim):
    return lax.broadcasted_iota(jnp.int32, shape, dim)


def ones_where(mask):
    return jnp.where(mask, 1.0, 0.0).astype(BF16)


def split3(x):
    hi = x.astype(BF16)
    rest = x - hi.astype(F32)
    mid = rest.astype(BF16)
    low = (rest - mid.astype(F32)).astype(BF16)
    return hi, mid, low


def rms(x):
    return x * lax.rsqrt(jnp.mean(x * x, axis=-1, keepdims=True) + EPS)


def gelu(x):
    return 0.5 * x * (1.0 + jnp.tanh(0.7978845608028654 * (x + 0.044715 * (x * x * x))))


def loop(start, stop, body):
    if stop - start <= UNROLL:
        for i in range(start, stop):
            body(i)
    else:
        def step(i, carry):
            body(i)
            return carry

        lax.fori_loop(start, stop, step, 0)


def log2(n):
    assert n & (n - 1) == 0
    return n.bit_length() - 1


def project_rest(normed, weight, joined):
    width = normed.shape[1]
    joined[:, width:] = dot(normed, weight[:, width:]).astype(BF16)


def project_queries(normed, weight, joined):
    width = normed.shape[1]
    joined[:, :width] = (dot(normed, weight[:, :width]) * HEAD_DIM**-0.5).astype(BF16)


def sums(decay, width):
    span = decay.shape[1]
    later = ones_where(iota((span, span), 0) >= iota((span, span), 1))
    earlier = ones_where(iota((span, span), 0) <= iota((span, span), 1))
    heads = ones_where(iota((width, MIXER_STREAMS), 0) // HEAD_DIM == iota((width, MIXER_STREAMS), 1))
    wide = jnp.zeros((span, width), F32)
    flat = jnp.zeros((MIXER_STREAMS, span), F32)
    for piece_of in split3(decay):
        wide = wide + dot_nt(later, dot(heads, piece_of).astype(BF16))
        flat = flat + dot(piece_of, earlier)
    return wide, flat


def kernel(
    seq, reps, owners,
    points, decay_one, decay_two, target, w_qkv_one, w_out_one, w_up, w_down, w_qkv_two, w_out_two,
    out,
    wq1, wo1, wq2, wo2, up, down,
    joined_one, joined_two, num_one, num_two, att_one, att_two,
    a_send, a_recv, b_send, b_recv, blk_send, blk_recv, acc,
    load_sem, own_sem, ring_send, ring_recv, core_send, core_recv, side_send, side_recv, pass_send, pass_recv,
    ex_send, ex_recv,
):
    me = lax.axis_index("seq")
    rep = lax.axis_index("rep")
    rows, width = points.shape
    rows_two = out.shape[0]
    half = seq // 2
    halves = 2 if reps % 2 == 0 else 1
    part = width // halves
    mine = rep % halves
    partner = rep + 1 - 2 * (rep % 2)
    quarters = 4 if reps % 4 == 0 else halves
    fine = width // quarters
    across = rep + 2 - 4 * ((rep // 2) % 2)
    crossing = quarters == 4
    neighbours = [partner] * (halves == 2) + [across] * crossing
    groups = width // LANES
    per_group = owners // groups
    state_rows = HEAD_DIM // per_group
    pair_rows = blk_send.shape[1]

    loads = [
        pltpu.make_async_copy(src, dst, load_sem.at[i])
        for i, (src, dst) in enumerate(
            ((w_qkv_one, wq1), (w_out_one, wo1), (w_qkv_two, wq2), (w_out_two, wo2))
        )
    ]
    loads[0].start()
    own = [
        pltpu.make_async_copy(w_up, up.at[me], own_sem.at[0]),
        pltpu.make_async_copy(w_down, down.at[me], own_sem.at[1]),
    ]

    barrier = pltpu.get_barrier_semaphore()

    def greet(i):
        pl.semaphore_signal(
            barrier, inc=1, device_id={"seq": lax.rem(me + i, seq)}, device_id_type=MESH
        )

    loop(1, seq, greet)
    for other in neighbours:
        pl.semaphore_signal(barrier, inc=1, device_id={"rep": other}, device_id_type=MESH)
    x = points[...].astype(F32)
    normed_one = rms(x).astype(BF16)
    wide, flat = sums(decay_one[...], width)
    pl.semaphore_wait(barrier, seq - 1 + len(neighbours))

    place = jnp.where(me % 2 == 0, me // 2, seq - 1 - me // 2)

    def at_place(p):
        q = lax.rem(p + 2 * seq, seq)
        return jnp.where(q < half, 2 * q, 2 * (seq - 1 - q) + 1)

    neighbour = (at_place(place + 1), at_place(place - 1))

    quarter = (rep % 2) * (quarters // 2) + (rep // 2) % 2 if crossing else mine

    def up_piece(s, index):
        return up.at[s, pl.ds(pl.multiple_of(index * fine, fine), fine), :]

    def piece(w, s):
        if w == 0:
            return up_piece(s, quarter)
        return down.at[s, :, pl.ds(pl.multiple_of(mine * part, part), part)]

    def own_piece(w):
        if w == 0:
            return w_up.at[pl.ds(pl.multiple_of(quarter * fine, fine), fine), :]
        return w_down.at[:, pl.ds(pl.multiple_of(mine * part, part), part)]

    def origin(way, k):
        return at_place(place - k if way == 0 else place + k)

    def ring(way, w, k, first=False):
        where = piece(w, me if first else origin(way, k - 1))
        return pltpu.make_async_remote_copy(
            src_ref=own_piece(w) if first else where,
            dst_ref=where,
            send_sem=ring_send.at[way, w, k - 1],
            recv_sem=ring_recv.at[way, w, k - 1],
            device_id={"seq": neighbour[way]},
            device_id_type=MESH,
        )

    def ring_arrival(way, w, k):
        where = piece(w, origin(way, k))
        return pltpu.make_async_remote_copy(
            src_ref=where,
            dst_ref=where,
            send_sem=ring_send.at[way, w, k - 1],
            recv_sem=ring_recv.at[way, w, k - 1],
            device_id={"seq": neighbour[way]},
            device_id_type=MESH,
        )

    def core(way, w, k):
        where = piece(w, origin(way, k))
        return pltpu.make_async_remote_copy(
            src_ref=where,
            dst_ref=where,
            send_sem=core_send.at[way, w, k - 1],
            recv_sem=core_recv.at[way, w, k - 1],
            device_id={"rep": partner},
            device_id_type=MESH,
        )

    def side(way, k):
        where = up_piece(origin(way, k), quarter)
        return pltpu.make_async_remote_copy(
            src_ref=where,
            dst_ref=where,
            send_sem=side_send.at[way, k - 1],
            recv_sem=side_recv.at[way, k - 1],
            device_id={"rep": across},
            device_id_type=MESH,
        )

    def side_arrival(way, k):
        where = up_piece(origin(way, k), quarter + 1 - 2 * (quarter % 2))
        return pltpu.make_async_remote_copy(
            src_ref=where,
            dst_ref=where,
            send_sem=side_send.at[way, k - 1],
            recv_sem=side_recv.at[way, k - 1],
            device_id={"rep": across},
            device_id_type=MESH,
        )

    def hand_on(way, k):
        where = up_piece(origin(way, k), quarter + 1 - 2 * (quarter % 2))
        return pltpu.make_async_remote_copy(
            src_ref=where,
            dst_ref=where,
            send_sem=pass_send.at[way, k - 1],
            recv_sem=pass_recv.at[way, k - 1],
            device_id={"rep": partner},
            device_id_type=MESH,
        )

    both = [(way, w) for w in range(2) for way in range(2)]
    last = [(0, 0), (1, 1)]

    def routes(k):
        return last if isinstance(k, int) and k == half else both

    def relay(k, routes_now, routes_next):
        for way, w in routes_now:
            ring_arrival(way, w, k).wait_recv()
            if (way, w) in routes_next:
                ring(way, w, k + 1).start()
            if crossing and w == 0:
                side(way, k).start()
            if halves == 2:
                core(way, w, k).start()

    def relay_part(k, w):
        relay(
            k,
            [route for route in routes(k) if route[1] == w],
            routes(k + 1) if k < half else [],
        )

    def crossed(k):
        if crossing:
            for way, w in routes(k):
                if w == 0:
                    side_arrival(way, k).wait_recv()
                    hand_on(way, k).start()

    for way, w in routes(1):
        ring(way, w, 1, first=True).start()
    for copy in loads[1:] + own:
        copy.start()

    def exchange(index, source, target_buf, place_in=()):
        def copy(i, peer):
            return pltpu.make_async_remote_copy(
                src_ref=source.at[(peer, *place_in)],
                dst_ref=target_buf.at[(me, *place_in)],
                send_sem=ex_send.at[index, i],
                recv_sem=ex_recv.at[index, i],
                device_id={"seq": peer},
                device_id_type=MESH,
            )

        def arrival(i):
            src = lax.rem(me - i + seq, seq)
            return pltpu.make_async_remote_copy(
                src_ref=target_buf.at[(src, *place_in)],
                dst_ref=target_buf.at[(src, *place_in)],
                send_sem=ex_send.at[index, i],
                recv_sem=ex_recv.at[index, i],
                device_id={"seq": lax.rem(me + i, seq)},
                device_id_type=MESH,
            )

        return copy, arrival

    def far_first(body):
        middle = seq // 2
        if seq <= UNROLL:
            for i in sorted(range(1, seq), key=lambda i: abs(i - middle)):
                body(i)
        else:
            loop(1, seq, body)

    def maybe(cond, all_true, body):
        if all_true:
            body()
        else:
            pl.when(cond)(body)

    def to_owners(index, layer, place_in=()):
        copy, arrival = exchange(index, a_send.at[layer], a_recv.at[layer], place_in)

        def start(i):
            peer = lax.rem(me + i, seq)
            maybe(peer < owners, owners == seq, lambda: copy(i, peer).start())

        def finish(i):
            peer = lax.rem(me + i, seq)
            maybe(me < owners, owners == seq, lambda: arrival(i).wait_recv())

        def sent(i):
            peer = lax.rem(me + i, seq)
            maybe(peer < owners, owners == seq, lambda: copy(i, peer).wait_send())

        return start, finish, sent

    def from_owners(index, layer):
        copy, arrival = exchange(index, b_send.at[layer], b_recv.at[layer])

        def start(i):
            peer = lax.rem(me + i, seq)
            maybe(me < owners, owners == seq, lambda: copy(i, peer).start())

        def finish(i):
            src = lax.rem(me - i + seq, seq)
            maybe(src < owners, owners == seq, lambda: arrival(i).wait_recv())

        def sent(i):
            peer = lax.rem(me + i, seq)
            maybe(me < owners, owners == seq, lambda: copy(i, peer).wait_send())

        return start, finish, sent

    def summarise(joined, wide, layer):
        span = joined.shape[0]
        total = wide[span - 1 : span, :]
        keys = (joined[:, width : 2 * width].astype(F32) * jnp.exp(total - wide)).astype(BF16)
        values = joined[:, 2 * width :]
        first_head = iota((HEAD_DIM, LANES), 1) < HEAD_DIM
        for g in range(groups):
            cols = slice(g * LANES, (g + 1) * LANES)
            state = dot_tn(keys[:, cols], values[:, cols])
            packed = jnp.where(first_head, state[:HEAD_DIM], state[HEAD_DIM:]).astype(BF16)
            for r in range(per_group):
                o = g * per_group + r
                a_send[layer, o, :state_rows] = packed[r * state_rows : (r + 1) * state_rows]

    def totals(wide, layer):
        span = wide.shape[0]
        total = wide[span - 1 : span, :]
        tail_row = iota((16, LANES), 0)
        for g in range(groups):
            cols = slice(g * LANES, (g + 1) * LANES)
            hi, mid, low = (jnp.broadcast_to(t.astype(F32), (16, LANES)) for t in split3(total[:, cols]))
            tail = jnp.where(tail_row == 0, hi, jnp.where(tail_row == 1, mid, jnp.where(tail_row == 2, low, 0.0)))
            for r in range(per_group):
                a_send[layer, g * per_group + r, state_rows:] = tail.astype(BF16)

    def own_summary(layer):
        maybe(me < owners, owners == seq, lambda: store(a_recv, layer, me, a_send[layer, me]))

    def store(ref, layer, index, value):
        ref[layer, index] = value

    def prefix(layer):
        def step(j, before):
            b_send[layer, j] = before.astype(BF16)
            message = a_recv[layer, j].astype(F32)
            total = message[state_rows : state_rows + 1] + message[state_rows + 1 : state_rows + 2]
            total = total + message[state_rows + 2 : state_rows + 3]
            return before * jnp.exp(total) + message[:state_rows]

        def run():
            before = jnp.zeros((state_rows, LANES), F32)
            if seq <= UNROLL:
                for j in range(seq):
                    before = step(j, before)
            else:
                lax.fori_loop(0, seq, step, before)
            b_recv[layer, me] = b_send[layer, me]

        maybe(me < owners, owners == seq, run)

    def inner(joined, wide, flat, num, g):
        span = joined.shape[0]
        cols = slice(g * LANES, (g + 1) * LANES)
        query = joined[:, cols]
        key = joined[:, width + g * LANES : width + (g + 1) * LANES]
        value = joined[:, 2 * width + g * LANES : 2 * width + (g + 1) * LANES]
        causal = iota((span, span), 0) >= iota((span, span), 1)
        total = jnp.zeros((span, LANES), F32)
        for a in range(2):
            mask = ones_where(iota((1, LANES), 1) // HEAD_DIM == a)
            h = 2 * g + a
            gap = wide[:, h * HEAD_DIM : h * HEAD_DIM + 1] - flat[h : h + 1, :]
            weight = jnp.exp(jnp.where(causal, gap, -1e30))
            scores = dot_nt(query, key * mask)
            total = total + dot((scores * weight).astype(BF16), value * mask)
        num[:, cols] = total

    def finish_heads(joined, grown, num, att, layer):
        same = ones_where(iota((LANES, LANES), 0) // HEAD_DIM == iota((LANES, LANES), 1) // HEAD_DIM)
        for g in range(groups):
            cols = slice(g * LANES, (g + 1) * LANES)
            packed = jnp.concatenate(
                [b_recv[layer, g * per_group + r] for r in range(per_group)], axis=0
            )
            entering = jnp.concatenate([packed, packed], axis=0) * same
            total = num[:, cols] + dot(joined[:, cols], entering) * grown[:, cols]
            mean = dot((total * total).astype(BF16), same) * (1.0 / HEAD_DIM)
            att[:, cols] = (total * lax.rsqrt(mean + EPS)).astype(BF16)

    loads[0].wait()
    project_rest(normed_one, wq1, joined_one)
    totals(wide, 0)
    summarise(joined_one, wide, 0)
    start, finish, sent_a1 = to_owners(0, 0)
    far_first(start)
    own_summary(0)
    project_queries(normed_one, wq1, joined_one)
    many = half > UNROLL // 2
    pumps = [] if many else [(k, w) for k in range(1, half + 1) for w in range(2)]

    def pump(count=1):
        for _ in range(min(count, len(pumps))):
            k, w = pumps.pop(0)
            relay_part(k, w)
            if w == 1:
                crossed(k)

    pump(2)
    for g in range(groups):
        inner(joined_one, wide, flat, num_one, g)
    loop(1, seq, finish)
    prefix(0)
    start, finish, sent_b1 = from_owners(1, 0)
    far_first(start)
    pump()

    blocks = target.shape[1]
    shift_cap, shift_row = log2(CAP), log2(BR)
    local_blocks = rows // BR
    shift_local = log2(local_blocks)
    slot = target[...]
    device_of = jnp.broadcast_to(lax.shift_right_logical(slot, shift_cap).astype(F32), (8, blocks)).astype(BF16)
    slot_in = lax.bitwise_and(slot, CAP - 1)
    token_block = iota((rows, blocks), 0) // BR + me * local_blocks
    pick = ones_where(token_block == iota((rows, blocks), 1))
    to_row = dot_nt(device_of, pick)[0:1]
    to_col = dot_nt(pick, device_of)[:, 0:1]
    t0, t1 = iota((rows, rows), 0), iota((rows, rows), 1)
    before = (t0 // BR < t1 // BR) & (t0 % BR == 0) & (to_row == to_col)
    rank = jnp.sum(jnp.where(before, 1.0, 0.0), axis=0, keepdims=True)
    send_row = to_row * pair_rows + rank * BR + (iota((1, rows), 1) % BR).astype(F32)
    all_rows = seq * pair_rows
    scatter = ones_where(iota((all_rows, rows), 0).astype(F32) == send_row)

    here = lax.shift_right_logical(slot, shift_cap) == me
    here_rows = ones_where(jnp.broadcast_to(here, (8, blocks)))
    chunk = min(LANES, blocks)
    c0, c1 = iota((chunk, chunk), 0), iota((chunk, chunk), 1)
    lower = ones_where((c0 // local_blocks == c1 // local_blocks) & (c1 < c0))
    same_index = ones_where(c0 == c1)
    placing = jnp.zeros((rows_two, all_rows), F32)
    used = jnp.zeros((8, rows_two), F32)
    row_slot = iota((rows_two, chunk), 0) // BR
    in_row = iota((chunk, all_rows), 1) // BR * BR
    for c in range(blocks // chunk):
        cols = slice(c * chunk, (c + 1) * chunk)
        rank_col = dot_nt(lower, here_rows[:, cols])[:, 0:1]
        here_col = dot_nt(same_index, here_rows[:, cols])[:, 0:1]
        block_col = (iota((chunk, 1), 0) + c * chunk) // local_blocks
        base = block_col.astype(F32) * pair_rows + rank_col * BR
        base = jnp.where(here_col > 0.5, base, -1.0)
        taken = ones_where((row_slot == slot_in[:, cols]) & here[:, cols])
        placing = placing + dot(taken, ones_where(base == in_row.astype(F32)))
        used = used + dot_nt(jnp.ones((8, chunk), BF16), taken)
    sub = iota((rows_two, all_rows), 0) % BR == iota((rows_two, all_rows), 1) % BR
    gather = jnp.where(sub, placing, 0.0).astype(BF16)
    wide_two, flat_two = sums(decay_two[...] * used[0:1], width)
    totals(wide_two, 1)
    start_tail, finish_tail, sent_tail = to_owners(5, 1, (pl.ds(state_rows, 16),))
    loop(1, seq, start_tail)
    pump()

    grown = jnp.exp(wide)
    loop(1, seq, finish)
    finish_heads(joined_one, grown, num_one, att_one, 0)
    loads[1].wait()
    first = (x + dot(att_one[...], wo1[...])).astype(BF16)
    normed = rms(first.astype(F32)).astype(BF16)

    def feed(s):
        hidden = gelu(dot(normed, up[s])).astype(BF16)
        acc[...] += dot(hidden, down[s])

    acc[...] = first.astype(F32)
    pump()
    for copy in own:
        copy.wait()
    feed(me)

    def take(k):
        if crossing:
            for way, w in routes(k):
                if w == 0:
                    hand_on(way, k).wait_recv()
        if halves == 2:
            for way, w in routes(k):
                core(way, w, k).wait_recv()
        feed(origin(0, k))
        if not (isinstance(k, int) and k == half):
            feed(origin(1, k))

    if many:
        loop(1, half - 1, lambda k: relay(k, both, both))
        relay(half - 1, both, last)
        relay(half, last, [])
        loop(1, half, crossed)
        crossed(half)
        loop(1, half, take)
        take(half)
    else:
        for k in range(1, half + 1):
            take(k)
            pump(1 if k == 1 else 2)
        assert not pumps

    layer_out = acc[...].astype(BF16)
    chosen = dot(scatter, layer_out).astype(BF16)
    for j in range(seq):
        blk_send[j] = chosen[j * pair_rows : (j + 1) * pair_rows]
    move, moved = exchange(2, blk_send, blk_recv)
    far_first(lambda i: move(i, lax.rem(me + i, seq)).start())
    blk_recv[me] = blk_send[me]
    loads[2].wait()
    loop(1, seq, finish_tail)
    loop(1, seq, lambda i: moved(i).wait_recv())
    placed = dot(gather, blk_recv[...].reshape(all_rows, width))

    normed_two = rms(placed).astype(BF16)
    project_rest(normed_two, wq2, joined_two)
    summarise(joined_two, wide_two, 1)
    start, finish, sent_a2 = to_owners(3, 1, (pl.ds(0, state_rows),))
    far_first(start)
    own_summary(1)
    project_queries(normed_two, wq2, joined_two)
    for g in range(groups // 2):
        inner(joined_two, wide_two, flat_two, num_two, g)
    loop(1, seq, finish)
    prefix(1)
    start, finish, sent_b2 = from_owners(4, 1)
    far_first(start)
    for g in range(groups // 2, groups):
        inner(joined_two, wide_two, flat_two, num_two, g)
    loads[3].wait()
    grown_two = jnp.exp(wide_two)

    for sent in (sent_a1, sent_b1, sent_tail, sent_a2):
        loop(1, seq, sent)
    loop(1, seq, lambda i: move(i, lax.rem(me + i, seq)).wait_send())
    for way, w in routes(1):
        ring(way, w, 1, first=True).wait_send()

    def relayed(k):
        for way, w in routes(k):
            if not (isinstance(k, int) and k == 1):
                ring(way, w, k).wait_send()
            if halves == 2:
                core(way, w, k).wait_send()
            if crossing and w == 0:
                side(way, k).wait_send()
                hand_on(way, k).wait_send()

    relayed(1)
    loop(2, half, relayed)
    relayed(half)
    loop(1, seq, finish)
    finish_heads(joined_two, grown_two, num_two, att_two, 1)
    out[...] = (placed + dot(att_two[...], wo2[...])).astype(BF16)
    loop(1, seq, sent_b2)


def shards(seq, reps, points, decay_one, decay_two, block_target, w_qkv_one, w_out_one, w_up, w_down, w_qkv_two, w_out_two):
    rows, width = points.shape
    rows_two = CAP * BR
    groups = width // LANES
    owners = min(seq, 4 * groups)
    state_rows = HEAD_DIM * groups // owners
    pair_rows = max(16, max(1, CAP // seq) * BR)
    half = seq // 2
    hidden = w_up.shape[1]
    vmem = pl.BlockSpec(memory_space=pltpu.VMEM)
    anywhere = pl.BlockSpec(memory_space=pl.ANY)
    dma = pltpu.SemaphoreType.DMA
    return pl.pallas_call(
        functools.partial(kernel, seq, reps, owners),
        out_shape=jax.ShapeDtypeStruct((rows_two, width), BF16),
        in_specs=[vmem] * 4 + [anywhere] * 6,
        out_specs=vmem,
        scratch_shapes=[
            pltpu.VMEM(w_qkv_one.shape, BF16),
            pltpu.VMEM(w_out_one.shape, BF16),
            pltpu.VMEM(w_qkv_two.shape, BF16),
            pltpu.VMEM(w_out_two.shape, BF16),
            pltpu.VMEM((seq, width, hidden), BF16),
            pltpu.VMEM((seq, hidden, width), BF16),
            pltpu.VMEM((rows, 3 * width), BF16),
            pltpu.VMEM((rows_two, 3 * width), BF16),
            pltpu.VMEM((rows, width), F32),
            pltpu.VMEM((rows_two, width), F32),
            pltpu.VMEM((rows, width), BF16),
            pltpu.VMEM((rows_two, width), BF16),
            pltpu.VMEM((2, owners, state_rows + 16, LANES), BF16),
            pltpu.VMEM((2, seq, state_rows + 16, LANES), BF16),
            pltpu.VMEM((2, seq, state_rows, LANES), BF16),
            pltpu.VMEM((2, owners, state_rows, LANES), BF16),
            pltpu.VMEM((seq, pair_rows, width), BF16),
            pltpu.VMEM((seq, pair_rows, width), BF16),
            pltpu.VMEM((rows, width), F32),
            dma((4,)),
            dma((2,)),
            dma((2, 2, half)),
            dma((2, 2, half)),
            dma((2, 2, half)),
            dma((2, 2, half)),
            dma((2, half)),
            dma((2, half)),
            dma((2, half)),
            dma((2, half)),
            dma((6, seq)),
            dma((6, seq)),
        ],
        compiler_params=pltpu.CompilerParams(
            collective_id=0, has_side_effects=True, vmem_limit_bytes=56 * 1024 * 1024
        ),
    )(
        points, decay_one, decay_two, block_target.reshape(1, -1),
        w_qkv_one, w_out_one, w_up, w_down, w_qkv_two, w_out_two,
    )


def solution(mesh):
    in_specs = (
        P(("rep", "seq"), None),
        P(None, ("rep", "seq")),
        P(None, ("rep", "seq")),
        P("rep"),
        P(),
        P(),
        P(None, "seq"),
        P("seq", None),
        P(),
        P(),
    )
    out_specs = P(("rep", "seq"), None)
    body = functools.partial(shards, mesh.shape["seq"], mesh.shape["rep"])
    return jax.shard_map(body, mesh=mesh, in_specs=in_specs, out_specs=out_specs, check_vma=False)
```

```python
import functools

import jax
import jax.numpy as jnp
from jax import lax
from jax.experimental import pallas as pl
from jax.experimental.pallas import tpu as pltpu
from jax.sharding import PartitionSpec as P

MIXER_STREAMS = 8
HEAD_DIM = 64
BR = 8
CAP = 32
LANES = 128
EPS = 1e-05
F32 = jnp.float32
BF16 = jnp.bfloat16
MESH = pl.DeviceIdType.MESH
UNROLL = 16


def dot(a, b):
    return jnp.dot(a, b, preferred_element_type=F32)


def dot_nt(a, b):
    return lax.dot_general(a, b, (((1,), (1,)), ((), ())), preferred_element_type=F32)


def dot_tn(a, b):
    return lax.dot_general(a, b, (((0,), (0,)), ((), ())), preferred_element_type=F32)


def iota(shape, dim):
    return lax.broadcasted_iota(jnp.int32, shape, dim)


def ones_where(mask):
    return jnp.where(mask, 1.0, 0.0).astype(BF16)


def split3(x):
    hi = x.astype(BF16)
    rest = x - hi.astype(F32)
    mid = rest.astype(BF16)
    low = (rest - mid.astype(F32)).astype(BF16)
    return hi, mid, low


def rms(x):
    return x * lax.rsqrt(jnp.mean(x * x, axis=-1, keepdims=True) + EPS)


def gelu(x):
    return 0.5 * x * (1.0 + jnp.tanh(0.7978845608028654 * (x + 0.044715 * (x * x * x))))


def loop(start, stop, body):
    if stop - start <= UNROLL:
        for i in range(start, stop):
            body(i)
    else:
        def step(i, carry):
            body(i)
            return carry

        lax.fori_loop(start, stop, step, 0)


def log2(n):
    assert n & (n - 1) == 0
    return n.bit_length() - 1


def strips(start, stop, size, body):
    def step(n, carry):
        body(pl.ds(pl.multiple_of(n * size, size), size))
        return carry

    lax.fori_loop(start // size, stop // size, step, 0)


def project_rest(normed, weight, joined):
    width = normed.shape[1]

    def strip(cols):
        joined[:, cols] = dot(normed, weight[:, cols]).astype(BF16)

    strips(width, 3 * width, 2 * LANES, strip)


def project_queries(normed, weight, joined):
    width = normed.shape[1]

    def strip(cols):
        joined[:, cols] = (dot(normed, weight[:, cols]) * HEAD_DIM**-0.5).astype(BF16)

    strips(0, width, 2 * LANES, strip)


def sums(decay, width):
    span = decay.shape[1]
    later = ones_where(iota((span, span), 0) >= iota((span, span), 1))
    earlier = ones_where(iota((span, span), 0) <= iota((span, span), 1))
    heads = ones_where(iota((width, MIXER_STREAMS), 0) // HEAD_DIM == iota((width, MIXER_STREAMS), 1))
    wide = jnp.zeros((span, width), F32)
    flat = jnp.zeros((MIXER_STREAMS, span), F32)
    for piece_of in split3(decay):
        wide = wide + dot_nt(later, dot(heads, piece_of).astype(BF16))
        flat = flat + dot(piece_of, earlier)
    return wide, flat


def kernel(
    seq, reps, owners,
    points, decay_one, decay_two, target, w_qkv_one, w_out_one, w_up, w_down, w_qkv_two, w_out_two,
    out,
    wq1, wo1, wq2, wo2, up, down,
    joined_one, joined_two, num_one, num_two, att_one, att_two,
    wide_one, wide_two, flat_one, flat_two, normed, held, a_send, a_recv, b_send, b_recv, blk_send, blk_recv, acc,
    load_sem, own_sem, ring_send, ring_recv, core_send, core_recv, side_send, side_recv, pass_send, pass_recv,
    ex_send, ex_recv,
):
    me = lax.axis_index("seq")
    rep = lax.axis_index("rep")
    rows, width = points.shape
    rows_two = out.shape[0]
    half = seq // 2
    halves = 2 if reps % 2 == 0 else 1
    part = width // halves
    mine = rep % halves
    partner = rep + 1 - 2 * (rep % 2)
    quarters = 4 if reps % 4 == 0 else halves
    fine = width // quarters
    across = rep + 2 - 4 * ((rep // 2) % 2)
    crossing = quarters == 4
    neighbours = [partner] * (halves == 2) + [across] * crossing
    groups = width // LANES
    per_group = owners // groups
    state_rows = HEAD_DIM // per_group
    pair_rows = blk_send.shape[1]

    loads = [
        pltpu.make_async_copy(src, dst, load_sem.at[i])
        for i, (src, dst) in enumerate(
            ((w_qkv_one, wq1), (w_out_one, wo1), (w_qkv_two, wq2), (w_out_two, wo2))
        )
    ]
    loads[0].start()
    own = [
        pltpu.make_async_copy(w_up, up.at[me], own_sem.at[0]),
        pltpu.make_async_copy(w_down, down.at[me], own_sem.at[1]),
    ]

    barrier = pltpu.get_barrier_semaphore()

    def greet(i):
        pl.semaphore_signal(
            barrier, inc=1, device_id={"seq": lax.rem(me + i, seq)}, device_id_type=MESH
        )

    loop(1, seq, greet)
    for other in neighbours:
        pl.semaphore_signal(barrier, inc=1, device_id={"rep": other}, device_id_type=MESH)
    x = points[...].astype(F32)
    normed_one = rms(x).astype(BF16)
    wide_one[...], flat_one[...] = sums(decay_one[...], width)
    pl.semaphore_wait(barrier, seq - 1 + len(neighbours))

    place = jnp.where(me % 2 == 0, me // 2, seq - 1 - me // 2)

    def at_place(p):
        q = lax.rem(p + 2 * seq, seq)
        return jnp.where(q < half, 2 * q, 2 * (seq - 1 - q) + 1)

    neighbour = (at_place(place + 1), at_place(place - 1))

    quarter = (rep % 2) * (quarters // 2) + (rep // 2) % 2 if crossing else mine

    def up_piece(s, index):
        return up.at[s, pl.ds(pl.multiple_of(index * fine, fine), fine), :]

    def piece(w, s):
        if w == 0:
            return up_piece(s, quarter)
        return down.at[s, :, pl.ds(pl.multiple_of(mine * part, part), part)]

    def own_piece(w):
        if w == 0:
            return w_up.at[pl.ds(pl.multiple_of(quarter * fine, fine), fine), :]
        return w_down.at[:, pl.ds(pl.multiple_of(mine * part, part), part)]

    def origin(way, k):
        return at_place(place + (2 * way - 1) * k)

    def ring(way, w, k, first=False):
        where = piece(w, me if first else origin(way, k - 1))
        return pltpu.make_async_remote_copy(
            src_ref=own_piece(w) if first else where,
            dst_ref=where,
            send_sem=ring_send.at[way, w, k - 1],
            recv_sem=ring_recv.at[way, w, k - 1],
            device_id={"seq": neighbour[way]},
            device_id_type=MESH,
        )

    def ring_arrival(way, w, k):
        where = piece(w, origin(way, k))
        return pltpu.make_async_remote_copy(
            src_ref=where,
            dst_ref=where,
            send_sem=ring_send.at[way, w, k - 1],
            recv_sem=ring_recv.at[way, w, k - 1],
            device_id={"seq": neighbour[way]},
            device_id_type=MESH,
        )

    def core(way, w, k):
        where = piece(w, origin(way, k))
        return pltpu.make_async_remote_copy(
            src_ref=where,
            dst_ref=where,
            send_sem=core_send.at[way, w, k - 1],
            recv_sem=core_recv.at[way, w, k - 1],
            device_id={"rep": partner},
            device_id_type=MESH,
        )

    def side(way, k):
        where = up_piece(origin(way, k), quarter)
        return pltpu.make_async_remote_copy(
            src_ref=where,
            dst_ref=where,
            send_sem=side_send.at[way, k - 1],
            recv_sem=side_recv.at[way, k - 1],
            device_id={"rep": across},
            device_id_type=MESH,
        )

    def side_arrival(way, k):
        where = up_piece(origin(way, k), quarter + 1 - 2 * (quarter % 2))
        return pltpu.make_async_remote_copy(
            src_ref=where,
            dst_ref=where,
            send_sem=side_send.at[way, k - 1],
            recv_sem=side_recv.at[way, k - 1],
            device_id={"rep": across},
            device_id_type=MESH,
        )

    def hand_on(way, k):
        where = up_piece(origin(way, k), quarter + 1 - 2 * (quarter % 2))
        return pltpu.make_async_remote_copy(
            src_ref=where,
            dst_ref=where,
            send_sem=pass_send.at[way, k - 1],
            recv_sem=pass_recv.at[way, k - 1],
            device_id={"rep": partner},
            device_id_type=MESH,
        )

    both = [(way, w) for w in range(2) for way in range(2)]
    last = [(0, 0), (1, 1)]

    def routes(k):
        return last if isinstance(k, int) and k == half else both

    def relay(k, routes_now, routes_next):
        for way, w in routes_now:
            ring_arrival(way, w, k).wait_recv()
            if (way, w) in routes_next:
                ring(way, w, k + 1).start()
            if crossing and w == 0:
                side(way, k).start()
            if halves == 2:
                core(way, w, k).start()

    def relay_part(k, w):
        relay(
            k,
            [route for route in routes(k) if route[1] == w],
            routes(k + 1) if k < half else [],
        )

    def crossed(k):
        if crossing:
            for way, w in routes(k):
                if w == 0:
                    side_arrival(way, k).wait_recv()
                    hand_on(way, k).start()

    for way, w in routes(1):
        ring(way, w, 1, first=True).start()
    for copy in loads[1:] + own:
        copy.start()

    def exchange(index, source, target_buf, place_in=()):
        def copy(i, peer):
            return pltpu.make_async_remote_copy(
                src_ref=source.at[(peer, *place_in)],
                dst_ref=target_buf.at[(me, *place_in)],
                send_sem=ex_send.at[index, i],
                recv_sem=ex_recv.at[index, i],
                device_id={"seq": peer},
                device_id_type=MESH,
            )

        def arrival(i):
            src = lax.rem(me - i + seq, seq)
            return pltpu.make_async_remote_copy(
                src_ref=target_buf.at[(src, *place_in)],
                dst_ref=target_buf.at[(src, *place_in)],
                send_sem=ex_send.at[index, i],
                recv_sem=ex_recv.at[index, i],
                device_id={"seq": lax.rem(me + i, seq)},
                device_id_type=MESH,
            )

        return copy, arrival

    def far_first(body):
        middle = seq // 2
        if seq <= UNROLL:
            for i in sorted(range(1, seq), key=lambda i: abs(i - middle)):
                body(i)
        else:
            loop(1, seq, body)

    def maybe(cond, all_true, body):
        if all_true:
            body()
        else:
            pl.when(cond)(body)

    def to_owners(index, layer, place_in=()):
        copy, arrival = exchange(index, a_send.at[layer], a_recv.at[layer], place_in)

        def start(i):
            peer = lax.rem(me + i, seq)
            maybe(peer < owners, owners == seq, lambda: copy(i, peer).start())

        def finish(i):
            peer = lax.rem(me + i, seq)
            maybe(me < owners, owners == seq, lambda: arrival(i).wait_recv())

        def sent(i):
            peer = lax.rem(me + i, seq)
            maybe(peer < owners, owners == seq, lambda: copy(i, peer).wait_send())

        return start, finish, sent

    def from_owners(index, layer):
        copy, arrival = exchange(index, b_send.at[layer], b_recv.at[layer])

        def start(i):
            peer = lax.rem(me + i, seq)
            maybe(me < owners, owners == seq, lambda: copy(i, peer).start())

        def finish(i):
            src = lax.rem(me - i + seq, seq)
            maybe(src < owners, owners == seq, lambda: arrival(i).wait_recv())

        def sent(i):
            peer = lax.rem(me + i, seq)
            maybe(me < owners, owners == seq, lambda: copy(i, peer).wait_send())

        return start, finish, sent

    def each_group(body, first=0, stop=groups):
        def step(g, carry):
            body(g, lambda start: pl.ds(pl.multiple_of(start + g * LANES, LANES), LANES))
            return carry

        lax.fori_loop(first, stop, step, 0)

    def summarise(joined, wide, layer):
        span = joined.shape[0]
        first_head = iota((HEAD_DIM, LANES), 1) < HEAD_DIM

        def group(g, cols):
            sums_here = wide[:, cols(0)]
            decay = jnp.exp(sums_here[span - 1 : span, :] - sums_here)
            keys = (joined[:, cols(width)].astype(F32) * decay).astype(BF16)
            state = dot_tn(keys, joined[:, cols(2 * width)])
            packed = jnp.where(first_head, state[:HEAD_DIM], state[HEAD_DIM:]).astype(BF16)
            for r in range(per_group):
                a_send[layer, g * per_group + r, :state_rows] = packed[r * state_rows : (r + 1) * state_rows]

        each_group(group)

    def totals(wide, layer):
        span = wide.shape[0]
        total = wide[span - 1 : span, :]
        tail_row = iota((16, LANES), 0)
        for g in range(groups):
            cols = slice(g * LANES, (g + 1) * LANES)
            hi, mid, low = (jnp.broadcast_to(t.astype(F32), (16, LANES)) for t in split3(total[:, cols]))
            tail = jnp.where(tail_row == 0, hi, jnp.where(tail_row == 1, mid, jnp.where(tail_row == 2, low, 0.0)))
            for r in range(per_group):
                a_send[layer, g * per_group + r, state_rows:] = tail.astype(BF16)

    def own_summary(layer):
        maybe(me < owners, owners == seq, lambda: store(a_recv, layer, me, a_send[layer, me]))

    def store(ref, layer, index, value):
        ref[layer, index] = value

    def prefix(layer):
        def step(j, before):
            b_send[layer, j] = before.astype(BF16)
            message = a_recv[layer, j].astype(F32)
            total = message[state_rows : state_rows + 1] + message[state_rows + 1 : state_rows + 2]
            total = total + message[state_rows + 2 : state_rows + 3]
            return before * jnp.exp(total) + message[:state_rows]

        def run():
            before = jnp.zeros((state_rows, LANES), F32)
            if seq <= UNROLL:
                for j in range(seq):
                    before = step(j, before)
            else:
                lax.fori_loop(0, seq, step, before)
            b_recv[layer, me] = b_send[layer, me]

        maybe(me < owners, owners == seq, run)

    def inner(joined, wide, flat, num, first=0, stop=groups):
        span = joined.shape[0]

        def group(g, cols):
            query = joined[:, cols(0)]
            key = joined[:, cols(width)]
            value = joined[:, cols(2 * width)]
            sums_here = wide[:, cols(0)]
            causal = iota((span, span), 0) >= iota((span, span), 1)
            total = jnp.zeros((span, LANES), F32)
            for a in range(2):
                mask = ones_where(iota((1, LANES), 1) // HEAD_DIM == a)
                gap = sums_here[:, a * HEAD_DIM : a * HEAD_DIM + 1] - flat[pl.ds(2 * g + a, 1), :]
                weight = jnp.exp(jnp.where(causal, gap, -1e30))
                scores = dot_nt(query, key * mask)
                total = total + dot((scores * weight).astype(BF16), value * mask)
            num[:, cols(0)] = total

        each_group(group, first, stop)

    def finish_heads(joined, wide, num, att, layer):
        same = ones_where(iota((LANES, LANES), 0) // HEAD_DIM == iota((LANES, LANES), 1) // HEAD_DIM)

        def group(g, cols):
            packed = jnp.concatenate(
                [b_recv[layer, g * per_group + r] for r in range(per_group)], axis=0
            )
            entering = jnp.concatenate([packed, packed], axis=0) * same
            total = num[:, cols(0)] + dot(joined[:, cols(0)], entering) * jnp.exp(wide[:, cols(0)])
            mean = dot((total * total).astype(BF16), same) * (1.0 / HEAD_DIM)
            att[:, cols(0)] = (total * lax.rsqrt(mean + EPS)).astype(BF16)

        each_group(group)

    loads[0].wait()
    project_rest(normed_one, wq1, joined_one)
    totals(wide_one, 0)
    summarise(joined_one, wide_one, 0)
    start, finish, sent_a1 = to_owners(0, 0)
    far_first(start)
    own_summary(0)
    project_queries(normed_one, wq1, joined_one)
    many = half > UNROLL // 2
    pumps = [] if many else [(k, w) for k in range(1, half + 1) for w in range(2)]

    def pump(count=1):
        for _ in range(min(count, len(pumps))):
            k, w = pumps.pop(0)
            relay_part(k, w)
            if w == 1:
                crossed(k)

    pump(2)
    inner(joined_one, wide_one, flat_one, num_one)
    loop(1, seq, finish)
    prefix(0)
    start, finish, sent_b1 = from_owners(1, 0)
    far_first(start)
    pump()

    blocks = target.shape[1]
    shift_cap, shift_row = log2(CAP), log2(BR)
    local_blocks = rows // BR
    shift_local = log2(local_blocks)
    slot = target[...]
    device_of = jnp.broadcast_to(lax.shift_right_logical(slot, shift_cap).astype(F32), (8, blocks)).astype(BF16)
    slot_in = lax.bitwise_and(slot, CAP - 1)
    token_block = iota((rows, blocks), 0) // BR + me * local_blocks
    pick = ones_where(token_block == iota((rows, blocks), 1))
    to_row = dot_nt(device_of, pick)[0:1]
    to_col = dot_nt(pick, device_of)[:, 0:1]
    t0, t1 = iota((rows, rows), 0), iota((rows, rows), 1)
    before = (t0 // BR < t1 // BR) & (t0 % BR == 0) & (to_row == to_col)
    rank = jnp.sum(jnp.where(before, 1.0, 0.0), axis=0, keepdims=True)
    send_row = to_row * pair_rows + rank * BR + (iota((1, rows), 1) % BR).astype(F32)
    all_rows = seq * pair_rows
    scatter = ones_where(iota((all_rows, rows), 0).astype(F32) == send_row)

    here = lax.shift_right_logical(slot, shift_cap) == me
    here_rows = ones_where(jnp.broadcast_to(here, (8, blocks)))
    chunk = min(LANES, blocks)
    c0, c1 = iota((chunk, chunk), 0), iota((chunk, chunk), 1)
    lower = ones_where((c0 // local_blocks == c1 // local_blocks) & (c1 < c0))
    same_index = ones_where(c0 == c1)
    placing = jnp.zeros((rows_two, all_rows), F32)
    used = jnp.zeros((8, rows_two), F32)
    row_slot = iota((rows_two, chunk), 0) // BR
    in_row = iota((chunk, all_rows), 1) // BR * BR
    for c in range(blocks // chunk):
        cols = slice(c * chunk, (c + 1) * chunk)
        rank_col = dot_nt(lower, here_rows[:, cols])[:, 0:1]
        here_col = dot_nt(same_index, here_rows[:, cols])[:, 0:1]
        block_col = (iota((chunk, 1), 0) + c * chunk) // local_blocks
        base = block_col.astype(F32) * pair_rows + rank_col * BR
        base = jnp.where(here_col > 0.5, base, -1.0)
        taken = ones_where((row_slot == slot_in[:, cols]) & here[:, cols])
        placing = placing + dot(taken, ones_where(base == in_row.astype(F32)))
        used = used + dot_nt(jnp.ones((8, chunk), BF16), taken)
    sub = iota((rows_two, all_rows), 0) % BR == iota((rows_two, all_rows), 1) % BR
    gather = jnp.where(sub, placing, 0.0).astype(BF16)
    wide_two[...], flat_two[...] = sums(decay_two[...] * used[0:1], width)
    totals(wide_two, 1)
    start_tail, finish_tail, sent_tail = to_owners(5, 1, (pl.ds(state_rows, 16),))
    loop(1, seq, start_tail)
    pump()

    loop(1, seq, finish)
    finish_heads(joined_one, wide_one, num_one, att_one, 0)
    loads[1].wait()
    first = (x + dot(att_one[...], wo1[...])).astype(BF16)
    normed[...] = rms(first.astype(F32)).astype(BF16)

    def feed(s):
        hidden = gelu(dot(normed[...], up[s])).astype(BF16)
        acc[...] += dot(hidden, down[s])

    acc[...] = first.astype(F32)
    pump()
    for copy in own:
        copy.wait()
    if many:
        loop(1, half - 1, lambda k: relay(k, both, both))
        relay(half - 1, both, last)
        relay(half, last, [])
        loop(1, half, crossed)
        crossed(half)

    def take(j, carry):
        k, way = (j + 1) // 2, lax.rem(j + 1, 2)

        @pl.when(jnp.logical_and(j > 0, j < seq - 1))
        def _():
            if halves == 2:
                core(way, 0, k).wait_recv()
                core(way, 1, k).wait_recv()
            if crossing:
                hand_on(way, k).wait_recv()

        @pl.when(j == seq - 1)
        def _():
            if halves == 2:
                core(0, 0, half).wait_recv()
                core(1, 1, half).wait_recv()
            if crossing:
                hand_on(0, half).wait_recv()

        feed(at_place(place + (2 * way - 1) * k))
        if not many:
            for count, after in ((1, seq // 4), (2, seq // 2)):
                pl.when(j == after)(functools.partial(pump, count))
        return carry

    lax.fori_loop(0, seq, take, 0)
    assert not pumps

    layer_out = acc[...].astype(BF16)
    chosen = dot(scatter, layer_out).astype(BF16)
    for j in range(seq):
        blk_send[j] = chosen[j * pair_rows : (j + 1) * pair_rows]
    move, moved = exchange(2, blk_send, blk_recv)
    far_first(lambda i: move(i, lax.rem(me + i, seq)).start())
    blk_recv[me] = blk_send[me]
    loads[2].wait()
    loop(1, seq, finish_tail)
    loop(1, seq, lambda i: moved(i).wait_recv())
    placed = dot(gather, blk_recv[...].reshape(all_rows, width))
    held[...] = placed

    normed_two = rms(placed).astype(BF16)
    project_rest(normed_two, wq2, joined_two)
    summarise(joined_two, wide_two, 1)
    start, finish, sent_a2 = to_owners(3, 1, (pl.ds(0, state_rows),))
    far_first(start)
    own_summary(1)
    project_queries(normed_two, wq2, joined_two)
    inner(joined_two, wide_two, flat_two, num_two, 0, groups // 2)
    loop(1, seq, finish)
    prefix(1)
    start, finish, sent_b2 = from_owners(4, 1)
    far_first(start)
    inner(joined_two, wide_two, flat_two, num_two, groups // 2, groups)
    loads[3].wait()

    for sent in (sent_a1, sent_b1, sent_tail, sent_a2):
        loop(1, seq, sent)
    loop(1, seq, lambda i: move(i, lax.rem(me + i, seq)).wait_send())
    for way, w in routes(1):
        ring(way, w, 1, first=True).wait_send()

    def relayed(k):
        for way, w in routes(k):
            if not (isinstance(k, int) and k == 1):
                ring(way, w, k).wait_send()
            if halves == 2:
                core(way, w, k).wait_send()
            if crossing and w == 0:
                side(way, k).wait_send()
                hand_on(way, k).wait_send()

    relayed(1)
    loop(2, half, relayed)
    relayed(half)
    loop(1, seq, finish)
    finish_heads(joined_two, wide_two, num_two, att_two, 1)

    def strip(cols):
        out[:, cols] = (held[:, cols] + dot(att_two[...], wo2[:, cols])).astype(BF16)

    strips(0, width, 2 * LANES, strip)
    loop(1, seq, sent_b2)


def shards(seq, reps, points, decay_one, decay_two, block_target, w_qkv_one, w_out_one, w_up, w_down, w_qkv_two, w_out_two):
    rows, width = points.shape
    rows_two = CAP * BR
    groups = width // LANES
    owners = min(seq, 4 * groups)
    state_rows = HEAD_DIM * groups // owners
    pair_rows = max(16, max(1, CAP // seq) * BR)
    half = seq // 2
    hidden = w_up.shape[1]
    vmem = pl.BlockSpec(memory_space=pltpu.VMEM)
    anywhere = pl.BlockSpec(memory_space=pl.ANY)
    dma = pltpu.SemaphoreType.DMA
    return pl.pallas_call(
        functools.partial(kernel, seq, reps, owners),
        out_shape=jax.ShapeDtypeStruct((rows_two, width), BF16),
        in_specs=[vmem] * 4 + [anywhere] * 6,
        out_specs=vmem,
        scratch_shapes=[
            pltpu.VMEM(w_qkv_one.shape, BF16),
            pltpu.VMEM(w_out_one.shape, BF16),
            pltpu.VMEM(w_qkv_two.shape, BF16),
            pltpu.VMEM(w_out_two.shape, BF16),
            pltpu.VMEM((seq, width, hidden), BF16),
            pltpu.VMEM((seq, hidden, width), BF16),
            pltpu.VMEM((rows, 3 * width), BF16),
            pltpu.VMEM((rows_two, 3 * width), BF16),
            pltpu.VMEM((rows, width), F32),
            pltpu.VMEM((rows_two, width), F32),
            pltpu.VMEM((rows, width), BF16),
            pltpu.VMEM((rows_two, width), BF16),
            pltpu.VMEM((rows, width), F32),
            pltpu.VMEM((rows_two, width), F32),
            pltpu.VMEM((MIXER_STREAMS, rows), F32),
            pltpu.VMEM((MIXER_STREAMS, rows_two), F32),
            pltpu.VMEM((rows, width), BF16),
            pltpu.VMEM((rows_two, width), F32),
            pltpu.VMEM((2, owners, state_rows + 16, LANES), BF16),
            pltpu.VMEM((2, seq, state_rows + 16, LANES), BF16),
            pltpu.VMEM((2, seq, state_rows, LANES), BF16),
            pltpu.VMEM((2, owners, state_rows, LANES), BF16),
            pltpu.VMEM((seq, pair_rows, width), BF16),
            pltpu.VMEM((seq, pair_rows, width), BF16),
            pltpu.VMEM((rows, width), F32),
            dma((4,)),
            dma((2,)),
            dma((2, 2, half)),
            dma((2, 2, half)),
            dma((2, 2, half)),
            dma((2, 2, half)),
            dma((2, half)),
            dma((2, half)),
            dma((2, half)),
            dma((2, half)),
            dma((6, seq)),
            dma((6, seq)),
        ],
        compiler_params=pltpu.CompilerParams(
            collective_id=0, has_side_effects=True, vmem_limit_bytes=56 * 1024 * 1024
        ),
    )(
        points, decay_one, decay_two, block_target.reshape(1, -1),
        w_qkv_one, w_out_one, w_up, w_down, w_qkv_two, w_out_two,
    )


def solution(mesh):
    in_specs = (
        P(("rep", "seq"), None),
        P(None, ("rep", "seq")),
        P(None, ("rep", "seq")),
        P("rep"),
        P(),
        P(),
        P(None, "seq"),
        P("seq", None),
        P(),
        P(),
    )
    out_specs = P(("rep", "seq"), None)
    body = functools.partial(shards, mesh.shape["seq"], mesh.shape["rep"])
    return jax.shard_map(body, mesh=mesh, in_specs=in_specs, out_specs=out_specs, check_vma=False)
```

```python
import functools

import jax
import jax.numpy as jnp
from jax import lax
from jax.experimental import pallas as pl
from jax.experimental.pallas import tpu as pltpu
from jax.sharding import PartitionSpec as P

MIXER_STREAMS = 8
HEAD_DIM = 64
BR = 8
CAP = 32
LANES = 128
EPS = 1e-05
F32 = jnp.float32
BF16 = jnp.bfloat16
MESH = pl.DeviceIdType.MESH
UNROLL = 16


def dot(a, b):
    return jnp.dot(a, b, preferred_element_type=F32)


def dot_nt(a, b):
    return lax.dot_general(a, b, (((1,), (1,)), ((), ())), preferred_element_type=F32)


def dot_tn(a, b):
    return lax.dot_general(a, b, (((0,), (0,)), ((), ())), preferred_element_type=F32)


def iota(shape, dim):
    return lax.broadcasted_iota(jnp.int32, shape, dim)


def ones_where(mask):
    return jnp.where(mask, 1.0, 0.0).astype(BF16)


def split3(x):
    hi = x.astype(BF16)
    rest = x - hi.astype(F32)
    mid = rest.astype(BF16)
    low = (rest - mid.astype(F32)).astype(BF16)
    return hi, mid, low


def rms(x):
    return x * lax.rsqrt(jnp.mean(x * x, axis=-1, keepdims=True) + EPS)


def gelu(x):
    return 0.5 * x * (1.0 + jnp.tanh(0.7978845608028654 * (x + 0.044715 * (x * x * x))))


def loop(start, stop, body):
    if stop - start <= UNROLL:
        for i in range(start, stop):
            body(i)
    else:
        def step(i, carry):
            body(i)
            return carry

        lax.fori_loop(start, stop, step, 0)


def log2(n):
    assert n & (n - 1) == 0
    return n.bit_length() - 1


def project_rest(normed, weight, joined):
    width = normed.shape[1]
    joined[:, width:] = dot(normed, weight[:, width:]).astype(BF16)


def project_queries(normed, weight, joined):
    width = normed.shape[1]
    joined[:, :width] = (dot(normed, weight[:, :width]) * HEAD_DIM**-0.5).astype(BF16)


def sums(decay, width):
    span = decay.shape[1]
    later = ones_where(iota((span, span), 0) >= iota((span, span), 1))
    earlier = ones_where(iota((span, span), 0) <= iota((span, span), 1))
    heads = ones_where(iota((width, MIXER_STREAMS), 0) // HEAD_DIM == iota((width, MIXER_STREAMS), 1))
    wide = jnp.zeros((span, width), F32)
    flat = jnp.zeros((MIXER_STREAMS, span), F32)
    for piece_of in split3(decay):
        wide = wide + dot_nt(later, dot(heads, piece_of).astype(BF16))
        flat = flat + dot(piece_of, earlier)
    return wide, flat


def kernel(
    seq, reps, owners,
    points_in, decay_one_in, decay_two_in, target_in,
    w_qkv_one, w_out_one, w_up, w_down, w_qkv_two, w_out_two,
    out,
    points, decay_one, decay_two, target,
    wq1, wo1, wq2, wo2, up, down,
    joined_one, joined_two, num_one, num_two, att_one, att_two,
    a_send, a_recv, b_send, b_recv, blk_send, blk_recv, acc,
    load_sem, own_sem, ring_send, ring_recv, core_send, core_recv, side_send, side_recv, pass_send, pass_recv,
    ex_send, ex_recv,
):
    me = lax.axis_index("seq")
    rep = lax.axis_index("rep")
    rows, width = points.shape
    rows_two = out.shape[0]
    half = seq // 2
    halves = 2 if reps % 2 == 0 else 1
    part = width // halves
    mine = rep % halves
    partner = rep + 1 - 2 * (rep % 2)
    quarters = 4 if reps % 4 == 0 else halves
    fine = width // quarters
    across = rep + 2 - 4 * ((rep // 2) % 2)
    crossing = quarters == 4
    neighbours = [partner] * (halves == 2) + [across] * crossing
    groups = width // LANES
    per_group = owners // groups
    state_rows = HEAD_DIM // per_group
    pair_rows = blk_send.shape[1]

    loads = [
        pltpu.make_async_copy(src, dst, load_sem.at[i])
        for i, (src, dst) in enumerate(
            ((w_qkv_one, wq1), (w_out_one, wo1), (w_qkv_two, wq2), (w_out_two, wo2))
        )
    ]
    small = [
        pltpu.make_async_copy(src, dst, load_sem.at[4 + i])
        for i, (src, dst) in enumerate(
            ((points_in, points), (decay_one_in, decay_one), (decay_two_in, decay_two), (target_in, target))
        )
    ]
    own = [
        pltpu.make_async_copy(w_up, up.at[me], own_sem.at[0]),
        pltpu.make_async_copy(w_down, down.at[me], own_sem.at[1]),
    ]

    barrier = pltpu.get_barrier_semaphore()

    def greet(i):
        pl.semaphore_signal(
            barrier, inc=1, device_id={"seq": lax.rem(me + i, seq)}, device_id_type=MESH
        )

    loop(1, seq, greet)
    for other in neighbours:
        pl.semaphore_signal(barrier, inc=1, device_id={"rep": other}, device_id_type=MESH)
    for copy in small:
        copy.start()
    loads[0].start()
    for copy in small:
        copy.wait()
    x = points[...].astype(F32)
    normed_one = rms(x).astype(BF16)
    wide, flat = sums(decay_one[...], width)
    pl.semaphore_wait(barrier, seq - 1 + len(neighbours))

    place = jnp.where(me % 2 == 0, me // 2, seq - 1 - me // 2)

    def at_place(p):
        q = lax.rem(p + 2 * seq, seq)
        return jnp.where(q < half, 2 * q, 2 * (seq - 1 - q) + 1)

    neighbour = (at_place(place + 1), at_place(place - 1))

    quarter = (rep % 2) * (quarters // 2) + (rep // 2) % 2 if crossing else mine

    def up_piece(s, index):
        return up.at[s, pl.ds(pl.multiple_of(index * fine, fine), fine), :]

    def piece(w, s):
        if w == 0:
            return up_piece(s, quarter)
        return down.at[s, :, pl.ds(pl.multiple_of(mine * part, part), part)]

    def own_piece(w):
        if w == 0:
            return w_up.at[pl.ds(pl.multiple_of(quarter * fine, fine), fine), :]
        return w_down.at[:, pl.ds(pl.multiple_of(mine * part, part), part)]

    def origin(way, k):
        return at_place(place - k if way == 0 else place + k)

    def ring(way, w, k, first=False):
        where = piece(w, me if first else origin(way, k - 1))
        return pltpu.make_async_remote_copy(
            src_ref=own_piece(w) if first else where,
            dst_ref=where,
            send_sem=ring_send.at[way, w, k - 1],
            recv_sem=ring_recv.at[way, w, k - 1],
            device_id={"seq": neighbour[way]},
            device_id_type=MESH,
        )

    def ring_arrival(way, w, k):
        where = piece(w, origin(way, k))
        return pltpu.make_async_remote_copy(
            src_ref=where,
            dst_ref=where,
            send_sem=ring_send.at[way, w, k - 1],
            recv_sem=ring_recv.at[way, w, k - 1],
            device_id={"seq": neighbour[way]},
            device_id_type=MESH,
        )

    def core(way, w, k):
        where = piece(w, origin(way, k))
        return pltpu.make_async_remote_copy(
            src_ref=where,
            dst_ref=where,
            send_sem=core_send.at[way, w, k - 1],
            recv_sem=core_recv.at[way, w, k - 1],
            device_id={"rep": partner},
            device_id_type=MESH,
        )

    def side(way, k):
        where = up_piece(origin(way, k), quarter)
        return pltpu.make_async_remote_copy(
            src_ref=where,
            dst_ref=where,
            send_sem=side_send.at[way, k - 1],
            recv_sem=side_recv.at[way, k - 1],
            device_id={"rep": across},
            device_id_type=MESH,
        )

    def side_arrival(way, k):
        where = up_piece(origin(way, k), quarter + 1 - 2 * (quarter % 2))
        return pltpu.make_async_remote_copy(
            src_ref=where,
            dst_ref=where,
            send_sem=side_send.at[way, k - 1],
            recv_sem=side_recv.at[way, k - 1],
            device_id={"rep": across},
            device_id_type=MESH,
        )

    def hand_on(way, k):
        where = up_piece(origin(way, k), quarter + 1 - 2 * (quarter % 2))
        return pltpu.make_async_remote_copy(
            src_ref=where,
            dst_ref=where,
            send_sem=pass_send.at[way, k - 1],
            recv_sem=pass_recv.at[way, k - 1],
            device_id={"rep": partner},
            device_id_type=MESH,
        )

    both = [(way, w) for w in range(2) for way in range(2)]
    last = [(0, 0), (1, 1)]

    def routes(k):
        return last if isinstance(k, int) and k == half else both

    def relay(k, routes_now, routes_next):
        for way, w in routes_now:
            ring_arrival(way, w, k).wait_recv()
            if (way, w) in routes_next:
                ring(way, w, k + 1).start()
            if crossing and w == 0:
                side(way, k).start()
            if halves == 2:
                core(way, w, k).start()

    def relay_part(k, w):
        relay(
            k,
            [route for route in routes(k) if route[1] == w],
            routes(k + 1) if k < half else [],
        )

    def crossed(k):
        if crossing:
            for way, w in routes(k):
                if w == 0:
                    side_arrival(way, k).wait_recv()
                    hand_on(way, k).start()

    for way, w in routes(1):
        ring(way, w, 1, first=True).start()
    for copy in loads[1:] + own:
        copy.start()

    def exchange(index, source, target_buf, place_in=()):
        def copy(i, peer):
            return pltpu.make_async_remote_copy(
                src_ref=source.at[(peer, *place_in)],
                dst_ref=target_buf.at[(me, *place_in)],
                send_sem=ex_send.at[index, i],
                recv_sem=ex_recv.at[index, i],
                device_id={"seq": peer},
                device_id_type=MESH,
            )

        def arrival(i):
            src = lax.rem(me - i + seq, seq)
            return pltpu.make_async_remote_copy(
                src_ref=target_buf.at[(src, *place_in)],
                dst_ref=target_buf.at[(src, *place_in)],
                send_sem=ex_send.at[index, i],
                recv_sem=ex_recv.at[index, i],
                device_id={"seq": lax.rem(me + i, seq)},
                device_id_type=MESH,
            )

        return copy, arrival

    def far_first(body):
        middle = seq // 2
        if seq <= UNROLL:
            for i in sorted(range(1, seq), key=lambda i: abs(i - middle)):
                body(i)
        else:
            loop(1, seq, body)

    def maybe(cond, all_true, body):
        if all_true:
            body()
        else:
            pl.when(cond)(body)

    def to_owners(index, layer, place_in=()):
        copy, arrival = exchange(index, a_send.at[layer], a_recv.at[layer], place_in)

        def start(i):
            peer = lax.rem(me + i, seq)
            maybe(peer < owners, owners == seq, lambda: copy(i, peer).start())

        def finish(i):
            peer = lax.rem(me + i, seq)
            maybe(me < owners, owners == seq, lambda: arrival(i).wait_recv())

        def sent(i):
            peer = lax.rem(me + i, seq)
            maybe(peer < owners, owners == seq, lambda: copy(i, peer).wait_send())

        return start, finish, sent

    def from_owners(index, layer):
        copy, arrival = exchange(index, b_send.at[layer], b_recv.at[layer])

        def start(i):
            peer = lax.rem(me + i, seq)
            maybe(me < owners, owners == seq, lambda: copy(i, peer).start())

        def finish(i):
            src = lax.rem(me - i + seq, seq)
            maybe(src < owners, owners == seq, lambda: arrival(i).wait_recv())

        def sent(i):
            peer = lax.rem(me + i, seq)
            maybe(me < owners, owners == seq, lambda: copy(i, peer).wait_send())

        return start, finish, sent

    def summarise(joined, wide, layer):
        span = joined.shape[0]
        total = wide[span - 1 : span, :]
        keys = (joined[:, width : 2 * width].astype(F32) * jnp.exp(total - wide)).astype(BF16)
        values = joined[:, 2 * width :]
        first_head = iota((HEAD_DIM, LANES), 1) < HEAD_DIM
        for g in range(groups):
            cols = slice(g * LANES, (g + 1) * LANES)
            state = dot_tn(keys[:, cols], values[:, cols])
            packed = jnp.where(first_head, state[:HEAD_DIM], state[HEAD_DIM:]).astype(BF16)
            for r in range(per_group):
                o = g * per_group + r
                a_send[layer, o, :state_rows] = packed[r * state_rows : (r + 1) * state_rows]

    def totals(wide, layer):
        span = wide.shape[0]
        total = wide[span - 1 : span, :]
        tail_row = iota((16, LANES), 0)
        for g in range(groups):
            cols = slice(g * LANES, (g + 1) * LANES)
            hi, mid, low = (jnp.broadcast_to(t.astype(F32), (16, LANES)) for t in split3(total[:, cols]))
            tail = jnp.where(tail_row == 0, hi, jnp.where(tail_row == 1, mid, jnp.where(tail_row == 2, low, 0.0)))
            for r in range(per_group):
                a_send[layer, g * per_group + r, state_rows:] = tail.astype(BF16)

    def own_summary(layer):
        maybe(me < owners, owners == seq, lambda: store(a_recv, layer, me, a_send[layer, me]))

    def store(ref, layer, index, value):
        ref[layer, index] = value

    def prefix(layer):
        def step(j, before):
            b_send[layer, j] = before.astype(BF16)
            message = a_recv[layer, j].astype(F32)
            total = message[state_rows : state_rows + 1] + message[state_rows + 1 : state_rows + 2]
            total = total + message[state_rows + 2 : state_rows + 3]
            return before * jnp.exp(total) + message[:state_rows]

        def run():
            before = jnp.zeros((state_rows, LANES), F32)
            if seq <= UNROLL:
                for j in range(seq):
                    before = step(j, before)
            else:
                lax.fori_loop(0, seq, step, before)
            b_recv[layer, me] = b_send[layer, me]

        maybe(me < owners, owners == seq, run)

    def inner(joined, wide, flat, num, g):
        span = joined.shape[0]
        cols = slice(g * LANES, (g + 1) * LANES)
        query = joined[:, cols]
        key = joined[:, width + g * LANES : width + (g + 1) * LANES]
        value = joined[:, 2 * width + g * LANES : 2 * width + (g + 1) * LANES]
        causal = iota((span, span), 0) >= iota((span, span), 1)
        total = jnp.zeros((span, LANES), F32)
        for a in range(2):
            mask = ones_where(iota((1, LANES), 1) // HEAD_DIM == a)
            h = 2 * g + a
            gap = wide[:, h * HEAD_DIM : h * HEAD_DIM + 1] - flat[h : h + 1, :]
            weight = jnp.exp(jnp.where(causal, gap, -1e30))
            scores = dot_nt(query, key * mask)
            total = total + dot((scores * weight).astype(BF16), value * mask)
        num[:, cols] = total

    def finish_heads(joined, grown, num, att, layer):
        same = ones_where(iota((LANES, LANES), 0) // HEAD_DIM == iota((LANES, LANES), 1) // HEAD_DIM)
        for g in range(groups):
            cols = slice(g * LANES, (g + 1) * LANES)
            packed = jnp.concatenate(
                [b_recv[layer, g * per_group + r] for r in range(per_group)], axis=0
            )
            entering = jnp.concatenate([packed, packed], axis=0) * same
            total = num[:, cols] + dot(joined[:, cols], entering) * grown[:, cols]
            mean = dot((total * total).astype(BF16), same) * (1.0 / HEAD_DIM)
            att[:, cols] = (total * lax.rsqrt(mean + EPS)).astype(BF16)

    loads[0].wait()
    project_rest(normed_one, wq1, joined_one)
    totals(wide, 0)
    summarise(joined_one, wide, 0)
    start, finish, sent_a1 = to_owners(0, 0)
    far_first(start)
    own_summary(0)
    project_queries(normed_one, wq1, joined_one)
    many = half > UNROLL // 2
    pumps = [] if many else [(k, w) for k in range(1, half + 1) for w in range(2)]

    def pump(count=1):
        for _ in range(min(count, len(pumps))):
            k, w = pumps.pop(0)
            relay_part(k, w)
            if w == 1:
                crossed(k)

    pump(2)
    for g in range(groups):
        inner(joined_one, wide, flat, num_one, g)
    loop(1, seq, finish)
    prefix(0)
    start, finish, sent_b1 = from_owners(1, 0)
    far_first(start)
    pump()

    blocks = target.shape[1]
    shift_cap, shift_row = log2(CAP), log2(BR)
    local_blocks = rows // BR
    shift_local = log2(local_blocks)
    slot = target[...]
    device_of = jnp.broadcast_to(lax.shift_right_logical(slot, shift_cap).astype(F32), (8, blocks)).astype(BF16)
    slot_in = lax.bitwise_and(slot, CAP - 1)
    token_block = iota((rows, blocks), 0) // BR + me * local_blocks
    pick = ones_where(token_block == iota((rows, blocks), 1))
    to_row = dot_nt(device_of, pick)[0:1]
    to_col = dot_nt(pick, device_of)[:, 0:1]
    t0, t1 = iota((rows, rows), 0), iota((rows, rows), 1)
    before = (t0 // BR < t1 // BR) & (t0 % BR == 0) & (to_row == to_col)
    rank = jnp.sum(jnp.where(before, 1.0, 0.0), axis=0, keepdims=True)
    send_row = to_row * pair_rows + rank * BR + (iota((1, rows), 1) % BR).astype(F32)
    all_rows = seq * pair_rows
    scatter = ones_where(iota((all_rows, rows), 0).astype(F32) == send_row)

    here = lax.shift_right_logical(slot, shift_cap) == me
    here_rows = ones_where(jnp.broadcast_to(here, (8, blocks)))
    chunk = min(LANES, blocks)
    c0, c1 = iota((chunk, chunk), 0), iota((chunk, chunk), 1)
    lower = ones_where((c0 // local_blocks == c1 // local_blocks) & (c1 < c0))
    same_index = ones_where(c0 == c1)
    placing = jnp.zeros((rows_two, all_rows), F32)
    used = jnp.zeros((8, rows_two), F32)
    row_slot = iota((rows_two, chunk), 0) // BR
    in_row = iota((chunk, all_rows), 1) // BR * BR
    for c in range(blocks // chunk):
        cols = slice(c * chunk, (c + 1) * chunk)
        rank_col = dot_nt(lower, here_rows[:, cols])[:, 0:1]
        here_col = dot_nt(same_index, here_rows[:, cols])[:, 0:1]
        block_col = (iota((chunk, 1), 0) + c * chunk) // local_blocks
        base = block_col.astype(F32) * pair_rows + rank_col * BR
        base = jnp.where(here_col > 0.5, base, -1.0)
        taken = ones_where((row_slot == slot_in[:, cols]) & here[:, cols])
        placing = placing + dot(taken, ones_where(base == in_row.astype(F32)))
        used = used + dot_nt(jnp.ones((8, chunk), BF16), taken)
    sub = iota((rows_two, all_rows), 0) % BR == iota((rows_two, all_rows), 1) % BR
    gather = jnp.where(sub, placing, 0.0).astype(BF16)
    wide_two, flat_two = sums(decay_two[...] * used[0:1], width)
    totals(wide_two, 1)
    start_tail, finish_tail, sent_tail = to_owners(5, 1, (pl.ds(state_rows, 16),))
    loop(1, seq, start_tail)
    pump()

    grown = jnp.exp(wide)
    loop(1, seq, finish)
    finish_heads(joined_one, grown, num_one, att_one, 0)
    loads[1].wait()
    first = (x + dot(att_one[...], wo1[...])).astype(BF16)

    chosen = dot(scatter, first).astype(BF16)
    for j in range(seq):
        blk_send[j] = chosen[j * pair_rows : (j + 1) * pair_rows]
    move, moved = exchange(2, blk_send, blk_recv)
    far_first(lambda i: move(i, lax.rem(me + i, seq)).start())
    blk_recv[me] = blk_send[me]
    pump(3)
    loop(1, seq, lambda i: moved(i).wait_recv())
    arrived = dot(gather, blk_recv[...].reshape(all_rows, width))
    normed = rms(arrived).astype(BF16)

    def feed(s):
        hidden = gelu(dot(normed, up[s])).astype(BF16)
        acc[...] += dot(hidden, down[s])

    acc[...] = arrived
    for copy in own:
        copy.wait()
    feed(me)

    def take(k):
        if crossing:
            for way, w in routes(k):
                if w == 0:
                    hand_on(way, k).wait_recv()
        if halves == 2:
            for way, w in routes(k):
                core(way, w, k).wait_recv()
        feed(origin(0, k))
        if not (isinstance(k, int) and k == half):
            feed(origin(1, k))

    if many:
        loop(1, half - 1, lambda k: relay(k, both, both))
        relay(half - 1, both, last)
        relay(half, last, [])
        loop(1, half, crossed)
        crossed(half)
        loop(1, half, take)
        take(half)
    else:
        for k in range(1, half + 1):
            take(k)
            pump(2)
        assert not pumps

    loads[2].wait()
    loop(1, seq, finish_tail)
    placed = acc[...].astype(BF16).astype(F32)

    normed_two = rms(placed).astype(BF16)
    project_rest(normed_two, wq2, joined_two)
    summarise(joined_two, wide_two, 1)
    start, finish, sent_a2 = to_owners(3, 1, (pl.ds(0, state_rows),))
    far_first(start)
    own_summary(1)
    project_queries(normed_two, wq2, joined_two)
    for g in range(groups // 2):
        inner(joined_two, wide_two, flat_two, num_two, g)
    loop(1, seq, finish)
    prefix(1)
    start, finish, sent_b2 = from_owners(4, 1)
    far_first(start)
    for g in range(groups // 2, groups):
        inner(joined_two, wide_two, flat_two, num_two, g)
    loads[3].wait()
    grown_two = jnp.exp(wide_two)

    for sent in (sent_a1, sent_b1, sent_tail, sent_a2):
        loop(1, seq, sent)
    loop(1, seq, lambda i: move(i, lax.rem(me + i, seq)).wait_send())
    for way, w in routes(1):
        ring(way, w, 1, first=True).wait_send()

    def relayed(k):
        for way, w in routes(k):
            if not (isinstance(k, int) and k == 1):
                ring(way, w, k).wait_send()
            if halves == 2:
                core(way, w, k).wait_send()
            if crossing and w == 0:
                side(way, k).wait_send()
                hand_on(way, k).wait_send()

    relayed(1)
    loop(2, half, relayed)
    relayed(half)
    loop(1, seq, finish)
    finish_heads(joined_two, grown_two, num_two, att_two, 1)
    out[...] = (placed + dot(att_two[...], wo2[...])).astype(BF16)
    loop(1, seq, sent_b2)


def shards(seq, reps, points, decay_one, decay_two, block_target, w_qkv_one, w_out_one, w_up, w_down, w_qkv_two, w_out_two):
    rows, width = points.shape
    rows_two = CAP * BR
    groups = width // LANES
    owners = min(seq, 4 * groups)
    state_rows = HEAD_DIM * groups // owners
    pair_rows = max(16, max(1, CAP // seq) * BR)
    half = seq // 2
    hidden = w_up.shape[1]
    vmem = pl.BlockSpec(memory_space=pltpu.VMEM)
    anywhere = pl.BlockSpec(memory_space=pl.ANY)
    dma = pltpu.SemaphoreType.DMA
    return pl.pallas_call(
        functools.partial(kernel, seq, reps, owners),
        out_shape=jax.ShapeDtypeStruct((rows_two, width), BF16),
        in_specs=[anywhere] * 10,
        out_specs=vmem,
        scratch_shapes=[
            pltpu.VMEM(points.shape, BF16),
            pltpu.VMEM(decay_one.shape, F32),
            pltpu.VMEM(decay_two.shape, F32),
            pltpu.VMEM((1, block_target.size), jnp.int32),
            pltpu.VMEM(w_qkv_one.shape, BF16),
            pltpu.VMEM(w_out_one.shape, BF16),
            pltpu.VMEM(w_qkv_two.shape, BF16),
            pltpu.VMEM(w_out_two.shape, BF16),
            pltpu.VMEM((seq, width, hidden), BF16),
            pltpu.VMEM((seq, hidden, width), BF16),
            pltpu.VMEM((rows, 3 * width), BF16),
            pltpu.VMEM((rows_two, 3 * width), BF16),
            pltpu.VMEM((rows, width), F32),
            pltpu.VMEM((rows_two, width), F32),
            pltpu.VMEM((rows, width), BF16),
            pltpu.VMEM((rows_two, width), BF16),
            pltpu.VMEM((2, owners, state_rows + 16, LANES), BF16),
            pltpu.VMEM((2, seq, state_rows + 16, LANES), BF16),
            pltpu.VMEM((2, seq, state_rows, LANES), BF16),
            pltpu.VMEM((2, owners, state_rows, LANES), BF16),
            pltpu.VMEM((seq, pair_rows, width), BF16),
            pltpu.VMEM((seq, pair_rows, width), BF16),
            pltpu.VMEM((rows_two, width), F32),
            dma((8,)),
            dma((2,)),
            dma((2, 2, half)),
            dma((2, 2, half)),
            dma((2, 2, half)),
            dma((2, 2, half)),
            dma((2, half)),
            dma((2, half)),
            dma((2, half)),
            dma((2, half)),
            dma((6, seq)),
            dma((6, seq)),
        ],
        compiler_params=pltpu.CompilerParams(
            collective_id=0, has_side_effects=True, vmem_limit_bytes=56 * 1024 * 1024
        ),
    )(
        points, decay_one, decay_two, block_target.reshape(1, -1),
        w_qkv_one, w_out_one, w_up, w_down, w_qkv_two, w_out_two,
    )


def solution(mesh):
    in_specs = (
        P(("rep", "seq"), None),
        P(None, ("rep", "seq")),
        P(None, ("rep", "seq")),
        P("rep"),
        P(),
        P(),
        P(None, "seq"),
        P("seq", None),
        P(),
        P(),
    )
    out_specs = P(("rep", "seq"), None)
    body = functools.partial(shards, mesh.shape["seq"], mesh.shape["rep"])
    return jax.shard_map(body, mesh=mesh, in_specs=in_specs, out_specs=out_specs, check_vma=False)
```
